32 devices in a mesh: layer: 8 (over y, x, core), plane: 4 (over z).
Axes of the slice: x: 2, y: 2, z: 4, core: 2. Of those that a mesh axis runs over, the one named last changes fastest.
Arguments:
- sources: bfloat16 [8, 8, 2, 128, 128], P('layer', 'plane'), may hold values from -6 to 6
- operator_tiles: float32 [8, 96, 2, 128, 128], P('layer', 'plane'), may hold values from -0.109375 to 0.109375
- tile_rows: int32 [8, 96], P('layer', 'plane'), may hold values from 0 to 1, as said below
- tile_cols: int32 [8, 96], P('layer', 'plane'), may hold values from 0 to 5, as said below
- send_blocks: int32 [4, 2, 1], P('plane'), may hold values from 0 to 1
Outputs:
- traces: float32 [8, 8, 2, 128, 128], P('layer', 'plane')
The draws below stay inside these ranges and needn't reach their ends.
Inputs may be any that keep to these rules, and one draw needn't show every extreme that they name: Entries of tile_rows lie in 0..1; in each layer and plane piece every row block has exactly 12 tiles, and among them at least one reads each of the four parts of the extended trace (arrived blocks, lower neighbour's, upper neighbour's, own trace). Entries of tile_cols index the extended trace of their piece.
All inputs are finite; a program needn't handle non-finite values.
Results may differ from the reference program's by a relative error of at most 0.0003.
Values sent between devices are 32-bit elements; how exact they have to be, the bound alone decides.
No kernel may reach another device: no remote copies, remote signals or barrier semaphores. Data moves between devices by JAX's collectives and lax.ppermute only.
A program may use at most 64 MiB of HBM per device.

```python
import jax
import jax.numpy as jnp
from jax import lax

BS = 128
NB = 2
NK = 1
TILES = 24
SHOTS = 128
TICKS = 3
LAYERS = 8
PIECES = 4
BLOCKS = 8
TILES_ALL = 96


def tile_pattern(key):
    key_order = jax.random.fold_in(key, 71)
    key_chosen = jax.random.fold_in(key, 72)
    count = LAYERS * PIECES
    positions = jnp.arange(TILES, dtype=jnp.int32)
    row_blocks = positions % NB
    category = positions // NB % 4
    chosen = jax.random.randint(key_chosen, (count, TILES), 0, NB * NK, dtype=jnp.int32)
    col_blocks = jnp.where(category[None, :] == 0, chosen % NB, jnp.where(category[None, :] == 1, NB + chosen % NK, jnp.where(category[None, :] == 2, NB + NK + chosen % NK, NB + 2 * NK + chosen % NB)))
    subkeys = jax.random.split(key_order, count)
    shuffle = jax.vmap(lambda one: jax.random.permutation(one, TILES))(subkeys)
    rows_out = jnp.take(row_blocks, shuffle, axis=0)
    cols_out = jnp.take_along_axis(col_blocks, shuffle, axis=1)
    return (rows_out.reshape(LAYERS, PIECES * TILES), cols_out.reshape(LAYERS, PIECES * TILES))


def draw_tile_rows(key, part):
    return tile_pattern(key)[0].astype(jnp.int32)


def draw_tile_cols(key, part):
    return tile_pattern(key)[1].astype(jnp.int32)


def with_ends(array, stream_key, least, top_value):
    place = [jax.random.randint(jax.random.fold_in(stream_key, axis), (), 0, length) for axis, length in enumerate(array.shape)]
    widest = array.shape.index(max(array.shape))
    next_to = place[:widest] + [(place[widest] + 1) % array.shape[widest]] + place[widest + 1:]
    return array.at[tuple(place)].set(least).at[tuple(next_to)].set(top_value)


def steps_of(stream_key, shape, cuts, smallest, high):
    level, own = 1.0, jax.random.fold_in(stream_key, 6)
    for axis_at, parts in cuts:
        steps = jnp.exp(jax.random.uniform(jax.random.fold_in(own, axis_at), (parts,), jnp.float32, smallest / len(cuts), high / len(cuts)))
        level = level * jnp.repeat(steps, shape[axis_at] // parts).reshape([-1 if axis == axis_at else 1 for axis in range(len(shape))])
    return level


def gaussian(key, dims, width, limit, cuts=(), held_as=jnp.bfloat16):
    values = jax.random.normal(key, dims, jnp.float32) * width
    if len(cuts) > 0:
        values = steps_of(key, dims, cuts, -0.22, 0.18) * values
    return jnp.clip(values, min=-limit, max=limit).astype(held_as)


def setup_inputs(seed: int = 0) -> dict:
    keys = jax.random.split(jax.random.key(seed), 6)
    return {
        "sources": gaussian(keys[0], (LAYERS, BLOCKS, 2, BS, SHOTS), 1.0, 6.0, ((0, 8), (1, 4))),
        "operator_tiles": gaussian(keys[1], (LAYERS, TILES_ALL, 2, BS, BS), (2 * BS * TILES // NB) ** -0.5, 0.109375, ((0, 8), (1, 4)), jnp.float32),
        "tile_rows": draw_tile_rows(jax.random.fold_in(keys[5], 71), 0),
        "tile_cols": draw_tile_cols(jax.random.fold_in(keys[5], 71), 0),
        "send_blocks": with_ends(jax.random.randint(keys[4], (PIECES, 2, NK), 0, NB), jax.random.fold_in(keys[4], 1), 0, NB - 1).astype(jnp.int32),
    }


def apply_piece(extended, mats, rows, cols):
    highest = lax.Precision.HIGHEST
    operands = jnp.take(extended, cols, axis=0)
    real_real = jnp.einsum('tij,tjs->tis', mats[:, 0], operands[:, 0], precision=highest)
    imag_imag = jnp.einsum('tij,tjs->tis', mats[:, 1], operands[:, 1], precision=highest)
    real_imag = jnp.einsum('tij,tjs->tis', mats[:, 0], operands[:, 1], precision=highest)
    imag_real = jnp.einsum('tij,tjs->tis', mats[:, 1], operands[:, 0], precision=highest)
    products = jnp.stack([real_real - imag_imag, real_imag + imag_real], axis=1)
    row_select = (rows[None, :] == jnp.arange(NB, dtype=jnp.int32)[:, None]).astype(products.dtype)
    return jnp.einsum('bt,tcis->bcis', row_select, products, precision=highest)


def reference(sources, operator_tiles, tile_rows, tile_cols, send_blocks):
    source_now = sources.astype(jnp.float32).reshape(LAYERS, PIECES, NB, 2, BS, SHOTS)
    mats_all = operator_tiles.reshape(LAYERS, PIECES, TILES, 2, BS, BS)
    rows_all = tile_rows.reshape(LAYERS, PIECES, TILES)
    cols_all = tile_cols.reshape(LAYERS, PIECES, TILES)
    traces = jnp.zeros_like(source_now)
    pieces_index = jnp.arange(PIECES, dtype=jnp.int32)[:, None]
    for repeat in range(TICKS):
        arrived = jnp.concatenate([jnp.zeros_like(traces[:1]), traces[:-1]], axis=0)
        to_lower = arrived[:, pieces_index, send_blocks[:, 0, :]]
        to_upper = arrived[:, pieces_index, send_blocks[:, 1, :]]
        blank = jnp.zeros_like(to_upper[:, :1])
        from_lower = jnp.concatenate([blank, to_upper[:, :-1]], axis=1)
        from_upper = jnp.concatenate([to_lower[:, 1:], blank], axis=1)
        extended = jnp.concatenate([arrived, from_lower, from_upper, traces], axis=2)

        def one_layer(packed):
            return jax.vmap(apply_piece)(*packed)

        fresh = lax.map(one_layer, (extended, mats_all, rows_all, cols_all))
        traces = fresh + source_now
    return traces.reshape(LAYERS, BLOCKS, 2, BS, SHOTS)
```

```python
import jax
import jax.numpy as jnp
from jax import lax
from jax.experimental import pallas as pl
from jax.experimental.pallas import tpu as pltpu
from jax.sharding import PartitionSpec as P

F32 = jnp.float32
BF16 = jnp.bfloat16
LIMIT = 40 * 1024 * 1024


def even_pair(p, planes):
    q = p + 1 if p % 2 == 0 else p - 1
    return q if q < planes else p


def odd_pair(p, planes):
    q = p - 1 if p % 2 == 0 else p + 1
    return q if 0 <= q < planes else p


def same(p, planes):
    return p


def to_next_layer(block, partner):
    layers = lax.axis_size("layer")
    planes = lax.axis_size("plane")
    route = [
        (l * planes + p, (l + 1) % layers * planes + partner(p, planes))
        for l in range(layers)
        for p in range(planes)
    ]
    return lax.ppermute(block, ("layer", "plane"), route)


def choose(send_ref, blocks_ref, even_ref, odd_ref):
    is_odd = lax.axis_index("plane") % 2
    listed = even_ref.shape[0]
    for k in range(listed):
        even_ref[k] = blocks_ref[send_ref[(1 - is_odd) * listed + k]].astype(F32)
        odd_ref[k] = blocks_ref[send_ref[is_odd * listed + k]].astype(F32)


def split(value):
    high = value.astype(BF16)
    return high, (value - high.astype(F32)).astype(BF16)


def operand(blocks):
    rows = []
    for real, imag in blocks:
        rows.append(jnp.concatenate([real, imag], axis=1))
        rows.append(jnp.concatenate([-imag, real], axis=1))
    return jnp.concatenate(rows, axis=0)


def product(a, b):
    return jnp.dot(a, b, preferred_element_type=F32)


def widen_kernel(send_ref, source_ref, all_ref, even_ref, odd_ref):
    all_ref[...] = source_ref[...].astype(F32)
    choose(send_ref, source_ref, even_ref, odd_ref)


def prepare_kernel(rows_ref, cols_ref, tiles_ref, source_ref, high_ref, low_ref, own_ref, total):
    tile_count, _, width, _ = tiles_ref.shape
    blocks_here = source_ref.shape[0]
    extended = total.shape[0] // blocks_here
    listed = (extended - 2 * blocks_here) // 2
    layer = lax.axis_index("layer")
    plane = lax.axis_index("plane")
    planes = lax.axis_size("plane")
    is_odd = plane % 2
    total[...] = jnp.zeros_like(total)

    def add(t, carry):
        col = cols_ref[t]
        is_lower = (col >= blocks_here) & (col < blocks_here + listed)
        is_upper = (col >= blocks_here + listed) & (col < blocks_here + 2 * listed)
        place = jnp.where(is_lower & (is_odd == 0), col + listed, col)
        place = jnp.where(is_upper & (is_odd == 0), col - listed, place)
        slot = rows_ref[t] * extended + place
        total[slot, :, :width] += tiles_ref[t, 0]
        total[slot, :, width:] += tiles_ref[t, 1]
        return carry

    lax.fori_loop(0, tile_count, add, 0, unroll=4)
    has_layer = layer > 0
    has_next = plane + 1 < planes
    has_even = has_layer & ((is_odd == 1) | has_next)
    has_odd = has_layer & jnp.where(is_odd == 1, has_next, plane > 0)
    for c in range(extended):
        keep = None
        if c < blocks_here:
            keep = has_layer
        elif c < blocks_here + listed:
            keep = has_even
        elif c < blocks_here + 2 * listed:
            keep = has_odd
        for r in range(blocks_here):
            value = total[r * extended + c]
            if keep is not None:
                value = jnp.where(keep, value, 0.0)
            high, low = split(value)
            here = (slice(r * width, (r + 1) * width), slice(c * 2 * width, (c + 1) * 2 * width))
            high_ref[here] = high
            low_ref[here] = low
    first = (extended - blocks_here) * 2 * width
    own = operand([(source_ref[b, 0], source_ref[b, 1]) for b in range(blocks_here)])
    result = product(high_ref[:, first:], own) + product(low_ref[:, first:], own)
    shots = source_ref.shape[3]
    for b in range(blocks_here):
        for part in range(2):
            own_ref[b, part] = (
                result[b * width : (b + 1) * width, part * shots : (part + 1) * shots]
                + source_ref[b, part].astype(F32)
            )


def gather(all_ref, even_ref, odd_ref):
    return [
        (ref[b, 0], ref[b, 1])
        for ref in (all_ref, even_ref, odd_ref)
        for b in range(ref.shape[0])
    ]


def store(result, base_ref, out_ref):
    blocks, _, width, shots = base_ref.shape
    for b in range(blocks):
        for part in range(2):
            out_ref[b, part] = (
                result[b * width : (b + 1) * width, part * shots : (part + 1) * shots]
                + base_ref[b, part].astype(F32)
            )


def middle_kernel(send_ref, high_ref, low_ref, own_ref, all_ref, even_ref, odd_ref, new_ref, new_even_ref, new_odd_ref):
    blocks = [(x.astype(BF16), y.astype(BF16)) for x, y in gather(all_ref, even_ref, odd_ref)]
    stacked = operand(blocks)
    depth = stacked.shape[0]
    result = product(high_ref[:, :depth], stacked) + product(low_ref[:, :depth], stacked)
    store(result, own_ref, new_ref)
    choose(send_ref, new_ref, new_even_ref, new_odd_ref)


def three_products(high_ref, low_ref, columns, blocks):
    halves = [(split(x), split(y)) for x, y in blocks]
    high = operand([(x[0], y[0]) for x, y in halves])
    low = operand([(x[1], y[1]) for x, y in halves])
    left = high_ref[:, columns]
    return product(left, high) + product(low_ref[:, columns], high) + product(left, low)


def own_kernel(high_ref, low_ref, source_ref, trace_ref, own_ref):
    blocks = [(trace_ref[b, 0], trace_ref[b, 1]) for b in range(trace_ref.shape[0])]
    depth = 2 * trace_ref.shape[2] * len(blocks)
    result = three_products(high_ref, low_ref, slice(high_ref.shape[1] - depth, None), blocks)
    store(result, source_ref, own_ref)


def last_kernel(high_ref, low_ref, own_ref, all_ref, even_ref, odd_ref, out_ref):
    blocks = gather(all_ref, even_ref, odd_ref)
    depth = 2 * all_ref.shape[2] * len(blocks)
    result = three_products(high_ref, low_ref, slice(0, depth), blocks)
    store(result, own_ref, out_ref)


def call(kernel, ins, outs, flops, scratch=()):
    moved = sum(x.size * x.dtype.itemsize for x in (*ins, *outs))
    smem = pl.BlockSpec(memory_space=pltpu.SMEM)
    vmem = pl.BlockSpec(memory_space=pltpu.VMEM)
    return pl.pallas_call(
        kernel,
        out_shape=outs,
        in_specs=[smem if x.dtype == jnp.int32 else vmem for x in ins],
        out_specs=[vmem] * len(outs),
        scratch_shapes=scratch,
        compiler_params=pltpu.CompilerParams(vmem_limit_bytes=LIMIT),
        cost_estimate=pl.CostEstimate(flops=flops, bytes_accessed=moved, transcendentals=0),
    )(*ins)


def per_device(sources, operator_tiles, tile_rows, tile_cols, send_blocks):
    source = sources[0]
    tiles = operator_tiles[0]
    send = send_blocks.reshape(-1)
    blocks, _, width, shots = source.shape
    listed = send_blocks.shape[2]
    extended = 2 * blocks + 2 * listed
    shape = jax.ShapeDtypeStruct
    trace = shape(source.shape, F32)
    part = shape((listed, 2, width, shots), F32)
    half = shape((blocks * width, extended * 2 * width), BF16)
    flops = 2 * blocks * width * extended * 2 * width * 2 * shots

    def exchange(whole, even, odd):
        return (
            to_next_layer(whole, same),
            to_next_layer(even, even_pair),
            to_next_layer(odd, odd_pair),
        )

    arrived = exchange(*call(widen_kernel, (send, source), (trace, part, part), 0))
    high, low, own = call(
        prepare_kernel,
        (tile_rows[0], tile_cols[0], tiles, source),
        (half, half, trace),
        flops,
        [pltpu.VMEM((blocks * extended, width, 2 * width), F32)],
    )
    traces, even, odd = call(
        middle_kernel, (send, high, low, own, *arrived), (trace, part, part), 2 * flops
    )
    arrived = exchange(traces, even, odd)
    (own,) = call(own_kernel, (high, low, source, traces), (trace,), flops)
    (out,) = call(last_kernel, (high, low, own, *arrived), (trace,), 2 * flops)
    return out[None]


def solution(mesh):
    placed = (
        P("layer", "plane", None, None, None),
        P("layer", "plane", None, None, None),
        P("layer", "plane"),
        P("layer", "plane"),
        P("plane", None, None),
    )
    return jax.shard_map(
        per_device,
        mesh=mesh,
        in_specs=placed,
        out_specs=P("layer", "plane", None, None, None),
        check_vma=False,
    )
```

```python
import jax
import jax.numpy as jnp
from jax import lax
from jax.experimental import pallas as pl
from jax.experimental.pallas import tpu as pltpu
from jax.sharding import PartitionSpec as P

F32 = jnp.float32
BF16 = jnp.bfloat16
LIMIT = 40 * 1024 * 1024
CHUNKS = 6


def even_pair(p, planes):
    q = p + 1 if p % 2 == 0 else p - 1
    return q if q < planes else p


def odd_pair(p, planes):
    q = p - 1 if p % 2 == 0 else p + 1
    return q if 0 <= q < planes else p


def same(p, planes):
    return p


def to_next_layer(block, partner):
    layers = lax.axis_size("layer")
    planes = lax.axis_size("plane")
    route = [
        (l * planes + p, (l + 1) % layers * planes + partner(p, planes))
        for l in range(layers)
        for p in range(planes)
    ]
    return lax.ppermute(block, ("layer", "plane"), route)


def split(value):
    high = value.astype(BF16)
    return high, (value - high.astype(F32)).astype(BF16)


def operand(blocks):
    rows = []
    for real, imag in blocks:
        rows.append(jnp.concatenate([real, imag], axis=1))
        rows.append(jnp.concatenate([-imag, real], axis=1))
    return jnp.concatenate(rows, axis=0)


def product(a, b):
    return jnp.dot(a, b, preferred_element_type=F32)


def two_products(matrix_ref, columns, operand_value):
    both = product(matrix_ref[:, columns], operand_value)
    half = both.shape[0] // 2
    return both[:half] + both[half:]


def three_products(matrix_ref, columns, blocks):
    halves = [(split(x), split(y)) for x, y in blocks]
    high = operand([(x[0], y[0]) for x, y in halves])
    low = operand([(x[1], y[1]) for x, y in halves])
    half = matrix_ref.shape[0] // 2
    return two_products(matrix_ref, columns, high) + product(matrix_ref[:half, columns], low)


def store(result, base_ref, out_ref):
    blocks, _, width, shots = base_ref.shape
    for b in range(blocks):
        for part in range(2):
            out_ref[b, part] = (
                result[b * width : (b + 1) * width, part * shots : (part + 1) * shots]
                + base_ref[b, part].astype(F32)
            )


def fetch(pairs, sems):
    copies = [pltpu.make_async_copy(a, b, sems.at[i]) for i, (a, b) in enumerate(pairs)]
    for copy in copies:
        copy.start()
    return copies


def widen_kernel(send_hbm, source_hbm, all_ref, even_ref, odd_ref, send_ref, source_ref, sems):
    copies = fetch([(source_hbm, source_ref), (send_hbm, send_ref)], sems)
    is_odd = lax.axis_index("plane") % 2
    listed = even_ref.shape[0]
    copies[0].wait()
    all_ref[...] = source_ref[...].astype(F32)
    copies[1].wait()
    for k in range(listed):
        even_ref[k] = source_ref[send_ref[(1 - is_odd) * listed + k]].astype(F32)
        odd_ref[k] = source_ref[send_ref[is_odd * listed + k]].astype(F32)


def prepare_kernel(
    rows_hbm, cols_hbm, send_hbm, source_hbm, tiles_hbm,
    matrix_ref, own_ref, mask_ref,
    rows_ref, cols_ref, send_ref, source_ref, tiles_ref, total, sems,
):
    tile_count, _, width, _ = tiles_ref.shape
    blocks_here = source_ref.shape[0]
    extended = total.shape[0] // blocks_here
    listed = (extended - 2 * blocks_here) // 2
    small = [(rows_hbm, rows_ref), (cols_hbm, cols_ref), (send_hbm, send_ref)]
    chunk = tile_count // CHUNKS if tile_count % CHUNKS == 0 else tile_count
    parts = [pl.ds(first, chunk) for first in range(0, tile_count, chunk)]
    large = [(tiles_hbm.at[part], tiles_ref.at[part]) for part in parts]
    copies = fetch(small + large + [(source_hbm, source_ref)], sems)
    layer = lax.axis_index("layer")
    plane = lax.axis_index("plane")
    planes = lax.axis_size("plane")
    is_odd = plane % 2
    total[...] = jnp.zeros_like(total)

    def add(t, carry):
        col = cols_ref[t]
        is_lower = (col >= blocks_here) & (col < blocks_here + listed)
        is_upper = (col >= blocks_here + listed) & (col < blocks_here + 2 * listed)
        place = jnp.where(is_lower & (is_odd == 0), col + listed, col)
        place = jnp.where(is_upper & (is_odd == 0), col - listed, place)
        slot = rows_ref[t] * extended + place
        total[slot, :, :width] += tiles_ref[t, 0]
        total[slot, :, width:] += tiles_ref[t, 1]
        return carry

    for copy in copies[:3]:
        copy.wait()
    for k in range(listed):
        to_even = send_ref[(1 - is_odd) * listed + k]
        to_odd = send_ref[is_odd * listed + k]
        for b in range(blocks_here):
            for kind, chosen in enumerate((to_even, to_odd)):
                mask_ref[kind, k, b] = jnp.full(mask_ref.shape[3:], jnp.where(chosen == b, 1.0, 0.0), F32)
    for i, copy in enumerate(copies[3:-1]):
        copy.wait()
        lax.fori_loop(i * chunk, (i + 1) * chunk, add, 0, unroll=True)
    has_layer = layer > 0
    has_next = plane + 1 < planes
    has_even = has_layer & ((is_odd == 1) | has_next)
    has_odd = has_layer & jnp.where(is_odd == 1, has_next, plane > 0)
    height = blocks_here * width
    for c in range(extended):
        keep = None
        if c < blocks_here:
            keep = has_layer
        elif c < blocks_here + listed:
            keep = has_even
        elif c < blocks_here + 2 * listed:
            keep = has_odd
        for r in range(blocks_here):
            value = total[r * extended + c]
            if keep is not None:
                value = jnp.where(keep, value, 0.0)
            high, low = split(value)
            here = slice(c * 2 * width, (c + 1) * 2 * width)
            matrix_ref[r * width : (r + 1) * width, here] = high
            matrix_ref[height + r * width : height + (r + 1) * width, here] = low
    copies[-1].wait()
    own = operand([(source_ref[b, 0], source_ref[b, 1]) for b in range(blocks_here)])
    columns = slice((extended - blocks_here) * 2 * width, None)
    store(two_products(matrix_ref, columns, own), source_ref, own_ref)


def gather(*refs):
    return [(ref[b, 0], ref[b, 1]) for ref in refs for b in range(ref.shape[0])]


def middle_kernel(mask_ref, matrix_ref, own_ref, all_ref, even_ref, odd_ref, new_ref, new_even_ref, new_odd_ref):
    blocks = [(x.astype(BF16), y.astype(BF16)) for x, y in gather(all_ref, even_ref, odd_ref)]
    stacked = operand(blocks)
    store(two_products(matrix_ref, slice(0, stacked.shape[0]), stacked), own_ref, new_ref)
    count, _, width, shots = new_ref.shape
    rows = mask_ref.shape[3]
    for kind, out_ref in enumerate((new_even_ref, new_odd_ref)):
        for k in range(out_ref.shape[0]):
            chosen = jnp.zeros((2, width // rows, rows, shots), F32)
            for b in range(count):
                block = new_ref[b].reshape(chosen.shape)
                chosen = jnp.where(mask_ref[kind, k, b][None, None] > 0.5, block, chosen)
            out_ref[k] = chosen.reshape(2, width, shots)


def own_kernel(matrix_ref, source_ref, trace_ref, own_ref):
    blocks = gather(trace_ref)
    depth = 2 * trace_ref.shape[2] * len(blocks)
    store(three_products(matrix_ref, slice(matrix_ref.shape[1] - depth, None), blocks), source_ref, own_ref)


def last_kernel(matrix_ref, own_ref, all_ref, even_ref, odd_ref, out_ref):
    blocks = gather(all_ref, even_ref, odd_ref)
    depth = 2 * all_ref.shape[2] * len(blocks)
    store(three_products(matrix_ref, slice(0, depth), blocks), own_ref, out_ref)


def call(kernel, ins, outs, flops, scratch=(), in_hbm=False):
    moved = sum(x.size * x.dtype.itemsize for x in (*ins, *outs))
    if in_hbm:
        ins = [pltpu.with_memory_space_constraint(x, pltpu.HBM) for x in ins]
    vmem = pl.BlockSpec(memory_space=pltpu.VMEM)
    hbm = pl.BlockSpec(memory_space=pltpu.HBM)
    return pl.pallas_call(
        kernel,
        out_shape=outs,
        in_specs=[hbm if in_hbm else vmem] * len(ins),
        out_specs=[vmem] * len(outs),
        scratch_shapes=scratch,
        compiler_params=pltpu.CompilerParams(vmem_limit_bytes=LIMIT),
        cost_estimate=pl.CostEstimate(flops=flops, bytes_accessed=moved, transcendentals=0),
    )(*ins)


def per_device(sources, operator_tiles, tile_rows, tile_cols, send_blocks):
    source = sources[0]
    tiles = operator_tiles[0]
    rows = tile_rows.reshape(-1)
    cols = tile_cols.reshape(-1)
    send = send_blocks.reshape(-1)
    blocks, _, width, shots = source.shape
    listed = send_blocks.shape[2]
    extended = 2 * blocks + 2 * listed
    shape = jax.ShapeDtypeStruct
    trace = shape(source.shape, F32)
    part = shape((listed, 2, width, shots), F32)
    matrix = shape((2 * blocks * width, extended * 2 * width), BF16)
    mask = shape((2, listed, blocks, 8, shots), F32)
    flops = 2 * blocks * width * extended * 2 * width * 2 * shots

    def exchange(whole, even, odd):
        return (
            to_next_layer(whole, same),
            to_next_layer(even, even_pair),
            to_next_layer(odd, odd_pair),
        )

    send_copy = pltpu.SMEM(send.shape, send.dtype)
    source_copy = pltpu.VMEM(source.shape, source.dtype)
    arrived = exchange(
        *call(
            widen_kernel,
            (send, source),
            (trace, part, part),
            0,
            [send_copy, source_copy, pltpu.SemaphoreType.DMA((2,))],
            in_hbm=True,
        )
    )
    matrix, own, mask = call(
        prepare_kernel,
        (rows, cols, send, source, tiles),
        (matrix, trace, mask),
        flops,
        [
            pltpu.SMEM(rows.shape, rows.dtype),
            pltpu.SMEM(cols.shape, cols.dtype),
            send_copy,
            source_copy,
            pltpu.VMEM(tiles.shape, F32),
            pltpu.VMEM((blocks * extended, width, 2 * width), F32),
            pltpu.SemaphoreType.DMA((CHUNKS + 4,)),
        ],
        in_hbm=True,
    )
    traces, even, odd = call(middle_kernel, (mask, matrix, own, *arrived), (trace, part, part), 2 * flops)
    arrived = exchange(traces, even, odd)
    (own,) = call(own_kernel, (matrix, source, traces), (trace,), flops)
    (out,) = call(last_kernel, (matrix, own, *arrived), (trace,), 2 * flops)
    return out[None]


def solution(mesh):
    placed = (
        P("layer", "plane", None, None, None),
        P("layer", "plane", None, None, None),
        P("layer", "plane"),
        P("layer", "plane"),
        P("plane", None, None),
    )
    return jax.shard_map(
        per_device,
        mesh=mesh,
        in_specs=placed,
        out_specs=P("layer", "plane", None, None, None),
        check_vma=False,
    )
```

```python
import jax
import jax.numpy as jnp
from jax import lax
from jax.experimental import pallas as pl
from jax.experimental.pallas import tpu as pltpu
from jax.sharding import PartitionSpec as P

F32 = jnp.float32
BF16 = jnp.bfloat16
LIMIT = 40 * 1024 * 1024
CHUNKS = 6


def even_pair(p, planes):
    q = p + 1 if p % 2 == 0 else p - 1
    return q if q < planes else p


def odd_pair(p, planes):
    q = p - 1 if p % 2 == 0 else p + 1
    return q if 0 <= q < planes else p


def same(p, planes):
    return p


def outward(l, p, layers, planes, partner):
    return (l + 1) % layers, partner(p, planes) if l % 2 == 1 and l + 1 < layers else p


def inward(l, p, layers, planes, partner):
    if l % 2 == 1:
        return l - 1, p
    return (l + 1, partner(p, planes)) if l + 1 < layers else (l, p)


def permute(block, way, partner):
    layers = lax.axis_size("layer")
    planes = lax.axis_size("plane")
    route = []
    for l in range(layers):
        for p in range(planes):
            to_layer, to_plane = way(l, p, layers, planes, partner)
            route.append((l * planes + p, to_layer * planes + to_plane))
    return lax.ppermute(block, ("layer", "plane"), route)


def onward(l, p, layers, planes, partner):
    return (l + 1) % layers, partner(p, planes) if l + 1 < layers else p


def split(value):
    high = value.astype(BF16)
    return high, (value - high.astype(F32)).astype(BF16)


def operand(blocks):
    rows = []
    for real, imag in blocks:
        rows.append(jnp.concatenate([real, imag], axis=1))
        rows.append(jnp.concatenate([-imag, real], axis=1))
    return jnp.concatenate(rows, axis=0)


def product(a, b):
    return jnp.dot(a, b, preferred_element_type=F32)


def two_products(matrix_ref, columns, operand_value):
    both = product(matrix_ref[:, columns], operand_value)
    half = both.shape[0] // 2
    return both[:half] + both[half:]


def three_products(matrix_ref, columns, blocks):
    halves = [(split(x), split(y)) for x, y in blocks]
    high = operand([(x[0], y[0]) for x, y in halves])
    low = operand([(x[1], y[1]) for x, y in halves])
    half = matrix_ref.shape[0] // 2
    return two_products(matrix_ref, columns, high) + product(matrix_ref[:half, columns], low)


def store(result, base_ref, out_ref):
    blocks, _, width, shots = base_ref.shape
    for b in range(blocks):
        for part in range(2):
            out_ref[b, part] = (
                result[b * width : (b + 1) * width, part * shots : (part + 1) * shots]
                + base_ref[b, part].astype(F32)
            )


def fetch(pairs, sems):
    copies = [pltpu.make_async_copy(a, b, sems.at[i]) for i, (a, b) in enumerate(pairs)]
    for copy in copies:
        copy.start()
    return copies


def widen_kernel(send_hbm, source_hbm, all_ref, even_ref, odd_ref, send_ref, source_ref, sems):
    copies = fetch([(source_hbm, source_ref), (send_hbm, send_ref)], sems)
    is_odd = lax.axis_index("plane") % 2
    listed = even_ref.shape[0]
    copies[0].wait()
    all_ref[...] = source_ref[...].astype(F32)
    copies[1].wait()
    for k in range(listed):
        even_ref[k] = source_ref[send_ref[(1 - is_odd) * listed + k]].astype(F32)
        odd_ref[k] = source_ref[send_ref[is_odd * listed + k]].astype(F32)


def prepare_kernel(
    rows_hbm, cols_hbm, send_hbm, source_hbm, tiles_hbm,
    matrix_ref, own_ref, mask_ref,
    rows_ref, cols_ref, send_ref, source_ref, tiles_ref, total, sems,
):
    tile_count, _, width, _ = tiles_ref.shape
    blocks_here = source_ref.shape[0]
    extended = total.shape[0] // blocks_here
    listed = (extended - 2 * blocks_here) // 2
    small = [(rows_hbm, rows_ref), (cols_hbm, cols_ref), (send_hbm, send_ref)]
    chunk = tile_count // CHUNKS if tile_count % CHUNKS == 0 else tile_count
    parts = [pl.ds(first, chunk) for first in range(0, tile_count, chunk)]
    large = [(tiles_hbm.at[part], tiles_ref.at[part]) for part in parts]
    copies = fetch(small + large + [(source_hbm, source_ref)], sems)
    layer = lax.axis_index("layer")
    plane = lax.axis_index("plane")
    planes = lax.axis_size("plane")
    is_odd = plane % 2
    total[...] = jnp.zeros_like(total)

    def add(t, carry):
        col = cols_ref[t]
        is_lower = (col >= blocks_here) & (col < blocks_here + listed)
        is_upper = (col >= blocks_here + listed) & (col < blocks_here + 2 * listed)
        place = jnp.where(is_lower & (is_odd == 0), col + listed, col)
        place = jnp.where(is_upper & (is_odd == 0), col - listed, place)
        slot = rows_ref[t] * extended + place
        total[slot, :, :width] += tiles_ref[t, 0]
        total[slot, :, width:] += tiles_ref[t, 1]
        return carry

    for copy in copies[:3]:
        copy.wait()
    for k in range(listed):
        to_even = send_ref[(1 - is_odd) * listed + k]
        to_odd = send_ref[is_odd * listed + k]
        for b in range(blocks_here):
            for kind, chosen in enumerate((to_even, to_odd)):
                mask_ref[kind, k, b] = jnp.full(mask_ref.shape[3:], jnp.where(chosen == b, 1.0, 0.0), F32)
    for i, copy in enumerate(copies[3:-1]):
        copy.wait()
        lax.fori_loop(i * chunk, (i + 1) * chunk, add, 0, unroll=True)
    has_layer = layer > 0
    has_next = plane + 1 < planes
    has_even = has_layer & ((is_odd == 1) | has_next)
    has_odd = has_layer & jnp.where(is_odd == 1, has_next, plane > 0)
    height = blocks_here * width
    for c in range(extended):
        keep = None
        if c < blocks_here:
            keep = has_layer
        elif c < blocks_here + listed:
            keep = has_even
        elif c < blocks_here + 2 * listed:
            keep = has_odd
        for r in range(blocks_here):
            value = total[r * extended + c]
            if keep is not None:
                value = jnp.where(keep, value, 0.0)
            high, low = split(value)
            here = slice(c * 2 * width, (c + 1) * 2 * width)
            matrix_ref[r * width : (r + 1) * width, here] = high
            matrix_ref[height + r * width : height + (r + 1) * width, here] = low
    copies[-1].wait()
    own = operand([(source_ref[b, 0], source_ref[b, 1]) for b in range(blocks_here)])
    columns = slice((extended - blocks_here) * 2 * width, None)
    store(two_products(matrix_ref, columns, own), source_ref, own_ref)


def gather(*refs):
    return [(ref[b, 0], ref[b, 1]) for ref in refs for b in range(ref.shape[0])]


def choose(mask_ref, new_ref, even_ref, odd_ref):
    count, _, width, shots = new_ref.shape
    rows = mask_ref.shape[3]
    for kind, out_ref in enumerate((even_ref, odd_ref)):
        for k in range(out_ref.shape[0]):
            chosen = jnp.zeros((2, width // rows, rows, shots), F32)
            for b in range(count):
                block = new_ref[b].reshape(chosen.shape)
                chosen = jnp.where(mask_ref[kind, k, b][None, None] > 0.5, block, chosen)
            out_ref[k] = chosen.reshape(2, width, shots)


def second_tick(matrix_ref, own_ref, arrived_refs, new_ref):
    blocks = [(x.astype(BF16), y.astype(BF16)) for x, y in gather(*arrived_refs)]
    stacked = operand(blocks)
    store(two_products(matrix_ref, slice(0, stacked.shape[0]), stacked), own_ref, new_ref)


def on_odd_layer():
    return lax.axis_index("layer") % 2 == 1


def odd_kernel(matrix_ref, own_ref, all_ref, even_ref, odd_ref, new_ref):
    @pl.when(on_odd_layer())
    def _():
        second_tick(matrix_ref, own_ref, (all_ref, even_ref, odd_ref), new_ref)

    @pl.when(jnp.logical_not(on_odd_layer()))
    def _():
        new_ref[...] = own_ref[...]


def even_kernel(mask_ref, matrix_ref, own_ref, known_ref, all_ref, even_ref, odd_ref, new_ref, new_even_ref, new_odd_ref):
    @pl.when(on_odd_layer())
    def _():
        new_ref[...] = known_ref[...]

    @pl.when(jnp.logical_not(on_odd_layer()))
    def _():
        second_tick(matrix_ref, own_ref, (all_ref, even_ref, odd_ref), new_ref)

    choose(mask_ref, new_ref, new_even_ref, new_odd_ref)


def own_kernel(matrix_ref, source_ref, trace_ref, own_ref):
    blocks = gather(trace_ref)
    depth = 2 * trace_ref.shape[2] * len(blocks)
    store(three_products(matrix_ref, slice(matrix_ref.shape[1] - depth, None), blocks), source_ref, own_ref)


def third_tick(matrix_ref, first, base_ref, refs, out_ref):
    blocks = gather(*refs)
    unit = 2 * base_ref.shape[2]
    columns = slice(first * unit, (first + len(blocks)) * unit)
    store(three_products(matrix_ref, columns, blocks), base_ref, out_ref)


def even_whole_kernel(matrix_ref, base_ref, all_ref, out_ref):
    @pl.when(on_odd_layer())
    def _():
        out_ref[...] = base_ref[...]

    @pl.when(jnp.logical_not(on_odd_layer()))
    def _():
        third_tick(matrix_ref, 0, base_ref, (all_ref,), out_ref)


def odd_whole_kernel(matrix_ref, base_ref, all_ref, out_ref):
    @pl.when(on_odd_layer())
    def _():
        third_tick(matrix_ref, 0, base_ref, (all_ref,), out_ref)

    @pl.when(jnp.logical_not(on_odd_layer()))
    def _():
        out_ref[...] = base_ref[...]


def last_kernel(matrix_ref, base_ref, even_ref, odd_ref, out_ref):
    third_tick(matrix_ref, base_ref.shape[0], base_ref, (even_ref, odd_ref), out_ref)


def call(kernel, ins, outs, flops, scratch=(), in_hbm=False, moved=None):
    if moved is None:
        moved = sum(x.size * x.dtype.itemsize for x in (*ins, *outs))
    if in_hbm:
        ins = [pltpu.with_memory_space_constraint(x, pltpu.HBM) for x in ins]
    vmem = pl.BlockSpec(memory_space=pltpu.VMEM)
    hbm = pl.BlockSpec(memory_space=pltpu.HBM)
    return pl.pallas_call(
        kernel,
        out_shape=outs,
        in_specs=[hbm if in_hbm else vmem] * len(ins),
        out_specs=[vmem] * len(outs),
        scratch_shapes=scratch,
        compiler_params=pltpu.CompilerParams(vmem_limit_bytes=LIMIT),
        cost_estimate=pl.CostEstimate(flops=flops, bytes_accessed=moved, transcendentals=0),
    )(*ins)


def per_device(sources, operator_tiles, tile_rows, tile_cols, send_blocks):
    source = sources[0]
    tiles = operator_tiles[0]
    rows = tile_rows.reshape(-1)
    cols = tile_cols.reshape(-1)
    send = send_blocks.reshape(-1)
    blocks, _, width, shots = source.shape
    listed = send_blocks.shape[2]
    extended = 2 * blocks + 2 * listed
    shape = jax.ShapeDtypeStruct
    trace = shape(source.shape, F32)
    part = shape((listed, 2, width, shots), F32)
    matrix = shape((2 * blocks * width, extended * 2 * width), BF16)
    mask = shape((2, listed, blocks, 8, shots), F32)
    flops = 2 * blocks * width * extended * 2 * width * 2 * shots

    send_copy = pltpu.SMEM(send.shape, send.dtype)
    source_copy = pltpu.VMEM(source.shape, source.dtype)
    whole, even, odd = call(
        widen_kernel,
        (send, source),
        (trace, part, part),
        0,
        [send_copy, source_copy, pltpu.SemaphoreType.DMA((2,))],
        in_hbm=True,
    )
    whole = permute(whole, onward, same)
    from_even = permute(even, inward, even_pair), permute(odd, inward, odd_pair)
    from_odd = permute(even, outward, even_pair), permute(odd, outward, odd_pair)
    matrix, own, mask = call(
        prepare_kernel,
        (rows, cols, send, source, tiles),
        (matrix, trace, mask),
        flops,
        [
            pltpu.SMEM(rows.shape, rows.dtype),
            pltpu.SMEM(cols.shape, cols.dtype),
            send_copy,
            source_copy,
            pltpu.VMEM(tiles.shape, F32),
            pltpu.VMEM((blocks * extended, width, 2 * width), F32),
            pltpu.SemaphoreType.DMA((CHUNKS + 4,)),
        ],
        in_hbm=True,
    )
    (second,) = call(odd_kernel, (matrix, own, whole, *from_even), (trace,), flops)
    early = permute(second, outward, same)
    traces, even, odd = call(
        even_kernel, (mask, matrix, own, second, whole, *from_odd), (trace, part, part), 10**11, moved=10**9
    )
    late = permute(traces, inward, same)
    even = permute(even, onward, even_pair)
    odd = permute(odd, onward, odd_pair)
    (own,) = call(own_kernel, (matrix, source, traces), (trace,), flops)
    (own,) = call(even_whole_kernel, (matrix, own, early), (trace,), 10**11, moved=10**9)
    (own,) = call(odd_whole_kernel, (matrix, own, late), (trace,), flops)
    (out,) = call(last_kernel, (matrix, own, even, odd), (trace,), flops)
    return out[None]


def solution(mesh):
    placed = (
        P("layer", "plane", None, None, None),
        P("layer", "plane", None, None, None),
        P("layer", "plane"),
        P("layer", "plane"),
        P("plane", None, None),
    )
    return jax.shard_map(
        per_device,
        mesh=mesh,
        in_specs=placed,
        out_specs=P("layer", "plane", None, None, None),
        check_vma=False,
    )
```

```python
import jax
import jax.numpy as jnp
from jax import lax
from jax.experimental import pallas as pl
from jax.experimental.pallas import tpu as pltpu
from jax.sharding import PartitionSpec as P

F32 = jnp.float32
BF16 = jnp.bfloat16
LIMIT = 40 * 1024 * 1024


def even_pair(p, planes):
    q = p + 1 if p % 2 == 0 else p - 1
    return q if q < planes else p


def odd_pair(p, planes):
    q = p - 1 if p % 2 == 0 else p + 1
    return q if 0 <= q < planes else p


def same(p, planes):
    return p


def outward(l, p, layers, planes, partner):
    return (l + 1) % layers, partner(p, planes) if l % 2 == 1 and l + 1 < layers else p


def inward(l, p, layers, planes, partner):
    if l % 2 == 1:
        return l - 1, p
    return (l + 1, partner(p, planes)) if l + 1 < layers else (l, p)


def permute(block, way, partner):
    layers = lax.axis_size("layer")
    planes = lax.axis_size("plane")
    route = []
    for l in range(layers):
        for p in range(planes):
            to_layer, to_plane = way(l, p, layers, planes, partner)
            route.append((l * planes + p, to_layer * planes + to_plane))
    return lax.ppermute(block, ("layer", "plane"), route)


def mixed(l, p, layers, planes, partner):
    if l + 1 == layers:
        return 0, p
    return l + 1, partner[l % 2](p, planes)


def onward(l, p, layers, planes, partner):
    return (l + 1) % layers, p


def split(value):
    high = value.astype(BF16)
    return high, (value - high.astype(F32)).astype(BF16)


def operand(blocks):
    rows = []
    for real, imag in blocks:
        rows.append(jnp.concatenate([real, imag], axis=1))
        rows.append(jnp.concatenate([-imag, real], axis=1))
    return jnp.concatenate(rows, axis=0)


def product(a, b):
    return jnp.dot(a, b, preferred_element_type=F32)


def two_products(matrix_ref, columns, operand_value):
    both = product(matrix_ref[:, columns], operand_value)
    half = both.shape[0] // 2
    return both[:half] + both[half:]


def three_products(matrix_ref, columns, blocks):
    halves = [(split(x), split(y)) for x, y in blocks]
    high = operand([(x[0], y[0]) for x, y in halves])
    low = operand([(x[1], y[1]) for x, y in halves])
    half = matrix_ref.shape[0] // 2
    return two_products(matrix_ref, columns, high) + product(matrix_ref[:half, columns], low)


def store(result, base_ref, out_ref):
    blocks, _, width, shots = base_ref.shape
    for b in range(blocks):
        for part in range(2):
            out_ref[b, part] = (
                result[b * width : (b + 1) * width, part * shots : (part + 1) * shots]
                + base_ref[b, part].astype(F32)
            )


def fetch(pairs, sems):
    copies = [pltpu.make_async_copy(a, b, sems.at[i]) for i, (a, b) in enumerate(pairs)]
    for copy in copies:
        copy.start()
    return copies


def widen_kernel(send_hbm, source_hbm, all_ref, even_ref, odd_ref, send_ref, source_ref, sems):
    copies = fetch([(source_hbm, source_ref), (send_hbm, send_ref)], sems)
    is_odd = lax.axis_index("plane") % 2
    listed = even_ref.shape[0]
    copies[0].wait()
    all_ref[...] = source_ref[...].astype(F32)
    copies[1].wait()
    for k in range(listed):
        even_ref[k] = source_ref[send_ref[(1 - is_odd) * listed + k]].astype(F32)
        odd_ref[k] = source_ref[send_ref[is_odd * listed + k]].astype(F32)


def prepare_kernel(
    rows_hbm, cols_hbm, send_hbm, source_hbm, tiles_ref,
    matrix_ref, own_ref, mask_ref,
    rows_ref, cols_ref, send_ref, source_ref, total, sems,
):
    tile_count, _, width, _ = tiles_ref.shape
    blocks_here = source_ref.shape[0]
    extended = total.shape[0] // blocks_here
    listed = (extended - 2 * blocks_here) // 2
    small = [(rows_hbm, rows_ref), (cols_hbm, cols_ref), (send_hbm, send_ref)]
    copies = fetch(small + [(source_hbm, source_ref)], sems)
    layer = lax.axis_index("layer")
    plane = lax.axis_index("plane")
    planes = lax.axis_size("plane")
    is_odd = plane % 2
    total[...] = jnp.zeros_like(total)

    def add(t, carry):
        col = cols_ref[t]
        is_lower = (col >= blocks_here) & (col < blocks_here + listed)
        is_upper = (col >= blocks_here + listed) & (col < blocks_here + 2 * listed)
        place = jnp.where(is_lower & (is_odd == 0), col + listed, col)
        place = jnp.where(is_upper & (is_odd == 0), col - listed, place)
        slot = rows_ref[t] * extended + place
        total[slot, :, :width] += tiles_ref[t, 0]
        total[slot, :, width:] += tiles_ref[t, 1]
        return carry

    for copy in copies[:3]:
        copy.wait()
    for k in range(listed):
        to_even = send_ref[(1 - is_odd) * listed + k]
        to_odd = send_ref[is_odd * listed + k]
        for b in range(blocks_here):
            for kind, chosen in enumerate((to_even, to_odd)):
                mask_ref[kind, k, b] = jnp.full(mask_ref.shape[3:], jnp.where(chosen == b, 1.0, 0.0), F32)
    lax.fori_loop(0, tile_count, add, 0, unroll=8)
    has_layer = layer > 0
    has_next = plane + 1 < planes
    has_even = has_layer & ((is_odd == 1) | has_next)
    has_odd = has_layer & jnp.where(is_odd == 1, has_next, plane > 0)
    height = blocks_here * width
    for c in range(extended):
        keep = None
        if c < blocks_here:
            keep = has_layer
        elif c < blocks_here + listed:
            keep = has_even
        elif c < blocks_here + 2 * listed:
            keep = has_odd
        for r in range(blocks_here):
            value = total[r * extended + c]
            if keep is not None:
                value = jnp.where(keep, value, 0.0)
            high, low = split(value)
            here = slice(c * 2 * width, (c + 1) * 2 * width)
            matrix_ref[r * width : (r + 1) * width, here] = high
            matrix_ref[height + r * width : height + (r + 1) * width, here] = low
    copies[-1].wait()
    own = operand([(source_ref[b, 0], source_ref[b, 1]) for b in range(blocks_here)])
    columns = slice((extended - blocks_here) * 2 * width, None)
    store(two_products(matrix_ref, columns, own), source_ref, own_ref)


def gather(*refs):
    return [(ref[b, 0], ref[b, 1]) for ref in refs for b in range(ref.shape[0])]


def choose(mask_ref, kind, new_ref, out_ref):
    count, _, width, shots = new_ref.shape
    rows = mask_ref.shape[3]
    for k in range(out_ref.shape[0]):
        chosen = jnp.zeros((2, width // rows, rows, shots), F32)
        for b in range(count):
            block = new_ref[b].reshape(chosen.shape)
            chosen = jnp.where(mask_ref[kind, k, b][None, None] > 0.5, block, chosen)
        out_ref[k] = chosen.reshape(2, width, shots)


def second_tick(matrix_ref, own_ref, arrived_refs, new_ref):
    blocks = [(x.astype(BF16), y.astype(BF16)) for x, y in gather(*arrived_refs)]
    stacked = operand(blocks)
    store(two_products(matrix_ref, slice(0, stacked.shape[0]), stacked), own_ref, new_ref)


def on_odd_layer():
    return lax.axis_index("layer") % 2 == 1


def odd_kernel(mask_ref, matrix_ref, own_ref, all_ref, even_ref, odd_ref, new_ref, new_even_ref):
    @pl.when(on_odd_layer())
    def _():
        second_tick(matrix_ref, own_ref, (all_ref, even_ref, odd_ref), new_ref)

    @pl.when(jnp.logical_not(on_odd_layer()))
    def _():
        new_ref[...] = own_ref[...]

    choose(mask_ref, 0, new_ref, new_even_ref)


def on_even_layer():
    layer = lax.axis_index("layer")
    return (layer % 2 == 0) & (layer > 0)


def even_kernel(mask_ref, matrix_ref, own_ref, known_ref, all_ref, even_ref, odd_ref, new_ref, mixed_ref, new_odd_ref):
    @pl.when(jnp.logical_not(on_even_layer()))
    def _():
        new_ref[...] = known_ref[...]

    @pl.when(on_even_layer())
    def _():
        second_tick(matrix_ref, own_ref, (all_ref, even_ref, odd_ref), new_ref)

    choose(mask_ref, 1, new_ref, new_odd_ref)

    @pl.when(on_odd_layer())
    def _():
        mixed_ref[...] = new_odd_ref[...]

    @pl.when(jnp.logical_not(on_odd_layer()))
    def _():
        choose(mask_ref, 0, new_ref, mixed_ref)


def own_kernel(matrix_ref, source_ref, trace_ref, own_ref):
    blocks = gather(trace_ref)
    depth = 2 * trace_ref.shape[2] * len(blocks)
    store(three_products(matrix_ref, slice(matrix_ref.shape[1] - depth, None), blocks), source_ref, own_ref)


def third_tick(matrix_ref, first, base_ref, refs, out_ref):
    blocks = gather(*refs)
    unit = 2 * base_ref.shape[2]
    columns = slice(first * unit, (first + len(blocks)) * unit)
    store(three_products(matrix_ref, columns, blocks), base_ref, out_ref)


def even_last_kernel(matrix_ref, base_ref, all_ref, even_ref, out_ref):
    @pl.when(jnp.logical_not(on_even_layer()))
    def _():
        out_ref[...] = base_ref[...]

    @pl.when(on_even_layer())
    def _():
        third_tick(matrix_ref, 0, base_ref, (all_ref, even_ref), out_ref)


def odd_whole_kernel(matrix_ref, base_ref, all_ref, out_ref):
    @pl.when(on_odd_layer())
    def _():
        third_tick(matrix_ref, 0, base_ref, (all_ref,), out_ref)

    @pl.when(jnp.logical_not(on_odd_layer()))
    def _():
        out_ref[...] = base_ref[...]


def last_kernel(matrix_ref, base_ref, mixed_ref, odd_ref, out_ref):
    blocks = base_ref.shape[0]

    @pl.when(on_odd_layer())
    def _():
        third_tick(matrix_ref, blocks, base_ref, (mixed_ref, odd_ref), out_ref)

    @pl.when(on_even_layer())
    def _():
        third_tick(matrix_ref, blocks + mixed_ref.shape[0], base_ref, (mixed_ref,), out_ref)

    @pl.when(lax.axis_index("layer") == 0)
    def _():
        out_ref[...] = base_ref[...]


def call(kernel, ins, outs, flops, scratch=(), in_hbm=False, moved=None):
    if moved is None:
        moved = sum(x.size * x.dtype.itemsize for x in (*ins, *outs))
    if in_hbm:
        ins = [x if x.size > 10**6 // 2 else pltpu.with_memory_space_constraint(x, pltpu.HBM) for x in ins]
    vmem = pl.BlockSpec(memory_space=pltpu.VMEM)
    hbm = pl.BlockSpec(memory_space=pltpu.HBM)
    return pl.pallas_call(
        kernel,
        out_shape=outs,
        in_specs=[hbm if in_hbm and x.size <= 10**6 // 2 else vmem for x in ins],
        out_specs=[vmem] * len(outs),
        scratch_shapes=scratch,
        compiler_params=pltpu.CompilerParams(vmem_limit_bytes=LIMIT),
        cost_estimate=pl.CostEstimate(flops=flops, bytes_accessed=moved, transcendentals=0),
    )(*ins)


def per_device(sources, operator_tiles, tile_rows, tile_cols, send_blocks):
    source = sources[0]
    tiles = operator_tiles[0]
    rows = tile_rows.reshape(-1)
    cols = tile_cols.reshape(-1)
    send = send_blocks.reshape(-1)
    blocks, _, width, shots = source.shape
    listed = send_blocks.shape[2]
    extended = 2 * blocks + 2 * listed
    shape = jax.ShapeDtypeStruct
    trace = shape(source.shape, F32)
    part = shape((listed, 2, width, shots), F32)
    matrix = shape((2 * blocks * width, extended * 2 * width), BF16)
    mask = shape((2, listed, blocks, 8, shots), F32)
    flops = 2 * blocks * width * extended * 2 * width * 2 * shots

    send_copy = pltpu.SMEM(send.shape, send.dtype)
    source_copy = pltpu.VMEM(source.shape, source.dtype)
    whole, even, odd = call(
        widen_kernel,
        (send, source),
        (trace, part, part),
        10**11,
        [send_copy, source_copy, pltpu.SemaphoreType.DMA((2,))],
        in_hbm=True,
        moved=10**8,
    )
    whole = permute(whole, onward, same)
    from_odd = permute(even, outward, even_pair), permute(odd, outward, odd_pair)
    from_even = permute(even, inward, even_pair), permute(odd, inward, odd_pair)
    matrix, own, mask = call(
        prepare_kernel,
        (rows, cols, send, source, tiles),
        (matrix, trace, mask),
        flops,
        [
            pltpu.SMEM(rows.shape, rows.dtype),
            pltpu.SMEM(cols.shape, cols.dtype),
            send_copy,
            source_copy,
            pltpu.VMEM((blocks * extended, width, 2 * width), F32),
            pltpu.SemaphoreType.DMA((4,)),
        ],
        in_hbm=True,
    )
    second, even = call(odd_kernel, (mask, matrix, own, whole, *from_even), (trace, part), flops)
    early = permute(second, outward, same)
    early_even = permute(even, outward, even_pair)
    traces, even, odd = call(
        even_kernel, (mask, matrix, own, second, whole, *from_odd), (trace, part, part), 2000000000, moved=0
    )
    late_mixed = permute(even, mixed, (even_pair, odd_pair))
    late_odd = permute(odd, inward, odd_pair)
    late = permute(traces, inward, same)
    (own,) = call(own_kernel, (matrix, source, traces), (trace,), flops)
    (own,) = call(even_last_kernel, (matrix, own, early, early_even), (trace,), 10**11, moved=10**9)
    (own,) = call(odd_whole_kernel, (matrix, own, late), (trace,), flops)
    (out,) = call(last_kernel, (matrix, own, late_mixed, late_odd), (trace,), flops)
    return out[None]


def solution(mesh):
    placed = (
        P("layer", "plane", None, None, None),
        P("layer", "plane", None, None, None),
        P("layer", "plane"),
        P("layer", "plane"),
        P("plane", None, None),
    )
    return jax.shard_map(
        per_device,
        mesh=mesh,
        in_specs=placed,
        out_specs=P("layer", "plane", None, None, None),
        check_vma=False,
    )
```

```python
import jax
import jax.numpy as jnp
from jax import lax
from jax.experimental import pallas as pl
from jax.experimental.pallas import tpu as pltpu
from jax.sharding import PartitionSpec as P

F32 = jnp.float32
BF16 = jnp.bfloat16
LIMIT = 40 * 1024 * 1024


def even_pair(p, planes):
    q = p + 1 if p % 2 == 0 else p - 1
    return q if q < planes else p


def odd_pair(p, planes):
    q = p - 1 if p % 2 == 0 else p + 1
    return q if 0 <= q < planes else p


def same(p, planes):
    return p


def outward(l, p, layers, planes, partner):
    return (l + 1) % layers, partner(p, planes) if l % 2 == 1 and l + 1 < layers else p


def inward(l, p, layers, planes, partner):
    if l % 2 == 1:
        return l - 1, p
    return (l + 1, partner(p, planes)) if l + 1 < layers else (l, p)


def permute(block, way, partner):
    layers = lax.axis_size("layer")
    planes = lax.axis_size("plane")
    route = []
    for l in range(layers):
        for p in range(planes):
            to_layer, to_plane = way(l, p, layers, planes, partner)
            route.append((l * planes + p, to_layer * planes + to_plane))
    return lax.ppermute(block, ("layer", "plane"), route)


def onward(l, p, layers, planes, partner):
    return (l + 1) % layers, p


def with_mate(block):
    layers = lax.axis_size("layer")
    if layers % 2:
        return permute(block, inward, same)[None]
    groups = [[l, l + 1] for l in range(0, layers, 2)]
    return lax.all_gather(block, "layer", axis_index_groups=groups)


def split(value):
    high = value.astype(BF16)
    return high, (value - high.astype(F32)).astype(BF16)


def operand(blocks):
    rows = []
    for real, imag in blocks:
        rows.append(jnp.concatenate([real, imag], axis=1))
        rows.append(jnp.concatenate([-imag, real], axis=1))
    return jnp.concatenate(rows, axis=0)


def product(a, b):
    return jnp.dot(a, b, preferred_element_type=F32)


def two_products(matrix_ref, columns, operand_value):
    both = product(matrix_ref[:, columns], operand_value)
    half = both.shape[0] // 2
    return both[:half] + both[half:]


def three_products(matrix_ref, columns, blocks):
    halves = [(split(x), split(y)) for x, y in blocks]
    high = operand([(x[0], y[0]) for x, y in halves])
    low = operand([(x[1], y[1]) for x, y in halves])
    half = matrix_ref.shape[0] // 2
    return two_products(matrix_ref, columns, high) + product(matrix_ref[:half, columns], low)


def store(result, base_ref, out_ref):
    blocks, _, width, shots = base_ref.shape
    for b in range(blocks):
        for part in range(2):
            out_ref[b, part] = (
                result[b * width : (b + 1) * width, part * shots : (part + 1) * shots]
                + base_ref[b, part].astype(F32)
            )


def fetch(pairs, sems):
    copies = [pltpu.make_async_copy(a, b, sems.at[i]) for i, (a, b) in enumerate(pairs)]
    for copy in copies:
        copy.start()
    return copies


def widen_kernel(send_hbm, source_hbm, all_ref, even_ref, odd_ref, send_ref, source_ref, sems):
    copies = fetch([(source_hbm, source_ref), (send_hbm, send_ref)], sems)
    is_odd = lax.axis_index("plane") % 2
    listed = even_ref.shape[0]
    copies[0].wait()
    all_ref[...] = source_ref[...].astype(F32)
    copies[1].wait()
    for k in range(listed):
        even_ref[k] = source_ref[send_ref[(1 - is_odd) * listed + k]].astype(F32)
        odd_ref[k] = source_ref[send_ref[is_odd * listed + k]].astype(F32)


def prepare_kernel(
    rows_hbm, cols_hbm, send_hbm, source_hbm, tiles_ref,
    matrix_ref, own_ref, mask_ref,
    rows_ref, cols_ref, send_ref, source_ref, total, sems,
):
    tile_count, _, width, _ = tiles_ref.shape
    blocks_here = source_ref.shape[0]
    extended = total.shape[0] // blocks_here
    listed = (extended - 2 * blocks_here) // 2
    small = [(rows_hbm, rows_ref), (cols_hbm, cols_ref), (send_hbm, send_ref)]
    copies = fetch(small + [(source_hbm, source_ref)], sems)
    layer = lax.axis_index("layer")
    plane = lax.axis_index("plane")
    planes = lax.axis_size("plane")
    is_odd = plane % 2
    total[...] = jnp.zeros_like(total)

    def add(t, carry):
        col = cols_ref[t]
        is_lower = (col >= blocks_here) & (col < blocks_here + listed)
        is_upper = (col >= blocks_here + listed) & (col < blocks_here + 2 * listed)
        place = jnp.where(is_lower & (is_odd == 0), col + listed, col)
        place = jnp.where(is_upper & (is_odd == 0), col - listed, place)
        slot = rows_ref[t] * extended + place
        total[slot, :, :width] += tiles_ref[t, 0]
        total[slot, :, width:] += tiles_ref[t, 1]
        return carry

    for copy in copies[:3]:
        copy.wait()
    for k in range(listed):
        to_even = send_ref[(1 - is_odd) * listed + k]
        to_odd = send_ref[is_odd * listed + k]
        for b in range(blocks_here):
            for kind, chosen in enumerate((to_even, to_odd)):
                mask_ref[kind, k, b] = jnp.full(mask_ref.shape[3:], jnp.where(chosen == b, 1.0, 0.0), F32)
    lax.fori_loop(0, tile_count, add, 0, unroll=8)
    has_layer = layer > 0
    has_next = plane + 1 < planes
    has_even = has_layer & ((is_odd == 1) | has_next)
    has_odd = has_layer & jnp.where(is_odd == 1, has_next, plane > 0)
    height = blocks_here * width
    for c in range(extended):
        keep = None
        if c < blocks_here:
            keep = has_layer
        elif c < blocks_here + listed:
            keep = has_even
        elif c < blocks_here + 2 * listed:
            keep = has_odd
        for r in range(blocks_here):
            value = total[r * extended + c]
            if keep is not None:
                value = jnp.where(keep, value, 0.0)
            high, low = split(value)
            here = slice(c * 2 * width, (c + 1) * 2 * width)
            matrix_ref[r * width : (r + 1) * width, here] = high
            matrix_ref[height + r * width : height + (r + 1) * width, here] = low
    copies[-1].wait()
    own = operand([(source_ref[b, 0], source_ref[b, 1]) for b in range(blocks_here)])
    columns = slice((extended - blocks_here) * 2 * width, None)
    store(two_products(matrix_ref, columns, own), source_ref, own_ref)


def gather(*refs):
    return [(ref[b, 0], ref[b, 1]) for ref in refs for b in range(ref.shape[0])]


def choose(mask_ref, kind, new_ref, out_ref):
    count, _, width, shots = new_ref.shape
    rows = mask_ref.shape[3]
    for k in range(out_ref.shape[0]):
        chosen = jnp.zeros((2, width // rows, rows, shots), F32)
        for b in range(count):
            block = new_ref[b].reshape(chosen.shape)
            chosen = jnp.where(mask_ref[kind, k, b][None, None] > 0.5, block, chosen)
        out_ref[k] = chosen.reshape(2, width, shots)


def second_tick(matrix_ref, own_ref, arrived_refs, new_ref):
    blocks = [(x.astype(BF16), y.astype(BF16)) for x, y in gather(*arrived_refs)]
    stacked = operand(blocks)
    store(two_products(matrix_ref, slice(0, stacked.shape[0]), stacked), own_ref, new_ref)


def on_odd_layer():
    return lax.axis_index("layer") % 2 == 1


def odd_kernel(mask_ref, matrix_ref, own_ref, all_ref, even_ref, odd_ref, new_ref, new_even_ref, new_odd_ref):
    @pl.when(on_odd_layer())
    def _():
        second_tick(matrix_ref, own_ref, (all_ref, even_ref, odd_ref), new_ref)

    @pl.when(jnp.logical_not(on_odd_layer()))
    def _():
        new_ref[...] = own_ref[...]

    choose(mask_ref, 0, new_ref, new_even_ref)
    choose(mask_ref, 1, new_ref, new_odd_ref)


def on_even_layer():
    layer = lax.axis_index("layer")
    return (layer % 2 == 0) & (layer > 0)


def even_kernel(mask_ref, matrix_ref, own_ref, known_ref, all_ref, even_ref, odd_ref, new_ref, new_even_ref, new_odd_ref):
    @pl.when(jnp.logical_not(on_even_layer()))
    def _():
        new_ref[...] = known_ref[...]

    @pl.when(on_even_layer())
    def _():
        second_tick(matrix_ref, own_ref, (all_ref, even_ref, odd_ref), new_ref)

    choose(mask_ref, 0, new_ref, new_even_ref)
    choose(mask_ref, 1, new_ref, new_odd_ref)


def own_kernel(matrix_ref, source_ref, trace_ref, own_ref):
    blocks = gather(trace_ref)
    depth = 2 * trace_ref.shape[2] * len(blocks)
    store(three_products(matrix_ref, slice(matrix_ref.shape[1] - depth, None), blocks), source_ref, own_ref)


def third_tick(matrix_ref, first, base_ref, refs, out_ref):
    blocks = gather(*refs)
    unit = 2 * base_ref.shape[2]
    columns = slice(first * unit, (first + len(blocks)) * unit)
    store(three_products(matrix_ref, columns, blocks), base_ref, out_ref)


def mate_kernel(matrix_ref, base_ref, pair_ref, out_ref):
    @pl.when(jnp.logical_not(on_odd_layer()))
    def _():
        out_ref[...] = base_ref[...]

    @pl.when(on_odd_layer())
    def _():
        third_tick(matrix_ref, 0, base_ref, (pair_ref.at[0],), out_ref)


def even_part_kernel(matrix_ref, base_ref, all_ref, even_ref, out_ref):
    @pl.when(jnp.logical_not(on_even_layer()))
    def _():
        out_ref[...] = base_ref[...]

    @pl.when(on_even_layer())
    def _():
        third_tick(matrix_ref, 0, base_ref, (all_ref, even_ref), out_ref)


def last_kernel(matrix_ref, base_ref, outer_odd_ref, inner_even_ref, inner_odd_ref, out_ref):
    blocks = base_ref.shape[0]

    @pl.when(on_odd_layer())
    def _():
        third_tick(matrix_ref, blocks, base_ref, (inner_even_ref, inner_odd_ref), out_ref)

    @pl.when(on_even_layer())
    def _():
        third_tick(matrix_ref, blocks + inner_even_ref.shape[0], base_ref, (outer_odd_ref,), out_ref)

    @pl.when(lax.axis_index("layer") == 0)
    def _():
        out_ref[...] = base_ref[...]


def call(kernel, ins, outs, flops, scratch=(), in_hbm=False, moved=None):
    if moved is None:
        moved = sum(x.size * x.dtype.itemsize for x in (*ins, *outs))
    if in_hbm:
        ins = [x if x.size > 10**6 // 2 else pltpu.with_memory_space_constraint(x, pltpu.HBM) for x in ins]
    vmem = pl.BlockSpec(memory_space=pltpu.VMEM)
    hbm = pl.BlockSpec(memory_space=pltpu.HBM)
    return pl.pallas_call(
        kernel,
        out_shape=outs,
        in_specs=[hbm if in_hbm and x.size <= 10**6 // 2 else vmem for x in ins],
        out_specs=[vmem] * len(outs),
        scratch_shapes=scratch,
        compiler_params=pltpu.CompilerParams(vmem_limit_bytes=LIMIT),
        cost_estimate=pl.CostEstimate(flops=flops, bytes_accessed=moved, transcendentals=0),
    )(*ins)


def per_device(sources, operator_tiles, tile_rows, tile_cols, send_blocks):
    source = sources[0]
    tiles = operator_tiles[0]
    rows = tile_rows.reshape(-1)
    cols = tile_cols.reshape(-1)
    send = send_blocks.reshape(-1)
    blocks, _, width, shots = source.shape
    listed = send_blocks.shape[2]
    extended = 2 * blocks + 2 * listed
    shape = jax.ShapeDtypeStruct
    trace = shape(source.shape, F32)
    part = shape((listed, 2, width, shots), F32)
    matrix = shape((2 * blocks * width, extended * 2 * width), BF16)
    mask = shape((2, listed, blocks, 8, shots), F32)
    flops = 2 * blocks * width * extended * 2 * width * 2 * shots

    send_copy = pltpu.SMEM(send.shape, send.dtype)
    source_copy = pltpu.VMEM(source.shape, source.dtype)
    whole, even, odd = call(
        widen_kernel,
        (send, source),
        (trace, part, part),
        10**11,
        [send_copy, source_copy, pltpu.SemaphoreType.DMA((2,))],
        in_hbm=True,
        moved=10**8,
    )
    whole = permute(whole, onward, same)
    from_odd = permute(even, outward, even_pair), permute(odd, outward, odd_pair)
    from_even = permute(even, inward, even_pair), permute(odd, inward, odd_pair)
    matrix, own, mask = call(
        prepare_kernel,
        (rows, cols, send, source, tiles),
        (matrix, trace, mask),
        flops,
        [
            pltpu.SMEM(rows.shape, rows.dtype),
            pltpu.SMEM(cols.shape, cols.dtype),
            send_copy,
            source_copy,
            pltpu.VMEM((blocks * extended, width, 2 * width), F32),
            pltpu.SemaphoreType.DMA((4,)),
        ],
        in_hbm=True,
    )
    second, even, odd = call(odd_kernel, (mask, matrix, own, whole, *from_even), (trace, part, part), flops)
    early = permute(second, outward, same), permute(even, outward, even_pair), permute(odd, outward, odd_pair)
    traces, even, odd = call(
        even_kernel, (mask, matrix, own, second, whole, *from_odd), (trace, part, part), flops)
    late_even = permute(even, inward, even_pair)
    late_odd = permute(odd, inward, odd_pair)
    pair = with_mate(traces)
    (own,) = call(own_kernel, (matrix, source, traces), (trace,), flops)
    (own,) = call(mate_kernel, (matrix, own, pair), (trace,), flops)
    (own,) = call(even_part_kernel, (matrix, own, *early[:2]), (trace,), 10**11, moved=10**9)
    (out,) = call(last_kernel, (matrix, own, early[2], late_even, late_odd), (trace,), flops)
    return out[None]


def solution(mesh):
    placed = (
        P("layer", "plane", None, None, None),
        P("layer", "plane", None, None, None),
        P("layer", "plane"),
        P("layer", "plane"),
        P("plane", None, None),
    )
    return jax.shard_map(
        per_device,
        mesh=mesh,
        in_specs=placed,
        out_specs=P("layer", "plane", None, None, None),
        check_vma=False,
    )
```

```python
import jax
import jax.numpy as jnp
from jax import lax
from jax.experimental import pallas as pl
from jax.experimental.pallas import tpu as pltpu
from jax.sharding import PartitionSpec as P

F32 = jnp.float32
BF16 = jnp.bfloat16
LIMIT = 40 * 1024 * 1024


def even_pair(p, planes):
    q = p + 1 if p % 2 == 0 else p - 1
    return q if q < planes else p


def odd_pair(p, planes):
    q = p - 1 if p % 2 == 0 else p + 1
    return q if 0 <= q < planes else p


def same(p, planes):
    return p


def outward(l, p, layers, planes, partner):
    return (l + 1) % layers, partner(p, planes) if l % 2 == 1 and l + 1 < layers else p


def inward(l, p, layers, planes, partner):
    if l % 2 == 1:
        return l - 1, p
    return (l + 1, partner(p, planes)) if l + 1 < layers else (l, p)


def permute(block, way, partner):
    layers = lax.axis_size("layer")
    planes = lax.axis_size("plane")
    route = []
    for l in range(layers):
        for p in range(planes):
            to_layer, to_plane = way(l, p, layers, planes, partner)
            route.append((l * planes + p, to_layer * planes + to_plane))
    return lax.ppermute(block, ("layer", "plane"), route)


def onward(l, p, layers, planes, partner):
    return (l + 1) % layers, p


def with_mate(block):
    layers = lax.axis_size("layer")
    if layers % 2:
        return permute(block, inward, same)[None]
    groups = [[l, l + 1] for l in range(0, layers, 2)]
    return lax.all_gather(block, "layer", axis_index_groups=groups)


def split(value):
    high = value.astype(BF16)
    return high, (value - high.astype(F32)).astype(BF16)


def operand(blocks):
    rows = []
    for real, imag in blocks:
        rows.append(jnp.concatenate([real, imag], axis=1))
        rows.append(jnp.concatenate([-imag, real], axis=1))
    return jnp.concatenate(rows, axis=0)


def product(a, b):
    return jnp.dot(a, b, preferred_element_type=F32)


def two_products(matrix_ref, columns, operand_value):
    both = product(matrix_ref[:, columns], operand_value)
    half = both.shape[0] // 2
    return both[:half] + both[half:]


def three_products(matrix_ref, columns, blocks):
    halves = [(split(x), split(y)) for x, y in blocks]
    high = operand([(x[0], y[0]) for x, y in halves])
    low = operand([(x[1], y[1]) for x, y in halves])
    half = matrix_ref.shape[0] // 2
    return two_products(matrix_ref, columns, high) + product(matrix_ref[:half, columns], low)


def store(result, base_ref, out_ref):
    blocks, _, width, shots = base_ref.shape
    for b in range(blocks):
        for part in range(2):
            out_ref[b, part] = (
                result[b * width : (b + 1) * width, part * shots : (part + 1) * shots]
                + base_ref[b, part].astype(F32)
            )


def fetch(pairs, sems):
    copies = [pltpu.make_async_copy(a, b, sems.at[i]) for i, (a, b) in enumerate(pairs)]
    for copy in copies:
        copy.start()
    return copies


def widen_kernel(send_hbm, source_hbm, all_ref, even_ref, odd_ref, send_ref, source_ref, sems):
    copies = fetch([(source_hbm, source_ref), (send_hbm, send_ref)], sems)
    is_odd = lax.axis_index("plane") % 2
    listed = even_ref.shape[0]
    copies[0].wait()
    all_ref[...] = source_ref[...].astype(F32)
    copies[1].wait()
    for k in range(listed):
        even_ref[k] = source_ref[send_ref[(1 - is_odd) * listed + k]].astype(F32)
        odd_ref[k] = source_ref[send_ref[is_odd * listed + k]].astype(F32)


def after_kernel(first_ref, payload_ref, passed_ref):
    passed_ref[...] = payload_ref[...]


def prepare_kernel(
    rows_hbm, cols_hbm, send_hbm, source_hbm, tiles_ref,
    matrix_ref, own_ref, mask_ref,
    rows_ref, cols_ref, send_ref, source_ref, total, sems,
):
    tile_count, _, width, _ = tiles_ref.shape
    blocks_here = source_ref.shape[0]
    extended = total.shape[0] // blocks_here
    listed = (extended - 2 * blocks_here) // 2
    small = [(rows_hbm, rows_ref), (cols_hbm, cols_ref), (send_hbm, send_ref)]
    copies = fetch(small + [(source_hbm, source_ref)], sems)
    layer = lax.axis_index("layer")
    plane = lax.axis_index("plane")
    planes = lax.axis_size("plane")
    is_odd = plane % 2
    total[...] = jnp.zeros_like(total)

    def add(t, carry):
        col = cols_ref[t]
        is_lower = (col >= blocks_here) & (col < blocks_here + listed)
        is_upper = (col >= blocks_here + listed) & (col < blocks_here + 2 * listed)
        place = jnp.where(is_lower & (is_odd == 0), col + listed, col)
        place = jnp.where(is_upper & (is_odd == 0), col - listed, place)
        slot = rows_ref[t] * extended + place
        total[slot, :, :width] += tiles_ref[t, 0]
        total[slot, :, width:] += tiles_ref[t, 1]
        return carry

    for copy in copies[:3]:
        copy.wait()
    for k in range(listed):
        to_even = send_ref[(1 - is_odd) * listed + k]
        to_odd = send_ref[is_odd * listed + k]
        for b in range(blocks_here):
            for kind, chosen in enumerate((to_even, to_odd)):
                mask_ref[kind, k, b] = jnp.full(mask_ref.shape[3:], jnp.where(chosen == b, 1.0, 0.0), F32)
    lax.fori_loop(0, tile_count, add, 0, unroll=8)
    has_layer = layer > 0
    has_next = plane + 1 < planes
    has_even = has_layer & ((is_odd == 1) | has_next)
    has_odd = has_layer & jnp.where(is_odd == 1, has_next, plane > 0)
    height = blocks_here * width
    for c in range(extended):
        keep = None
        if c < blocks_here:
            keep = has_layer
        elif c < blocks_here + listed:
            keep = has_even
        elif c < blocks_here + 2 * listed:
            keep = has_odd
        for r in range(blocks_here):
            value = total[r * extended + c]
            if keep is not None:
                value = jnp.where(keep, value, 0.0)
            high, low = split(value)
            here = slice(c * 2 * width, (c + 1) * 2 * width)
            matrix_ref[r * width : (r + 1) * width, here] = high
            matrix_ref[height + r * width : height + (r + 1) * width, here] = low
    copies[-1].wait()
    own = operand([(source_ref[b, 0], source_ref[b, 1]) for b in range(blocks_here)])
    columns = slice((extended - blocks_here) * 2 * width, None)
    store(two_products(matrix_ref, columns, own), source_ref, own_ref)


def gather(*refs):
    return [(ref[b, 0], ref[b, 1]) for ref in refs for b in range(ref.shape[0])]


def choose(mask_ref, kind, new_ref, out_ref):
    count, _, width, shots = new_ref.shape
    rows = mask_ref.shape[3]
    for k in range(out_ref.shape[0]):
        chosen = jnp.zeros((2, width // rows, rows, shots), F32)
        for b in range(count):
            block = new_ref[b].reshape(chosen.shape)
            chosen = jnp.where(mask_ref[kind, k, b][None, None] > 0.5, block, chosen)
        out_ref[k] = chosen.reshape(2, width, shots)


def second_tick(matrix_ref, own_ref, arrived_refs, new_ref):
    blocks = [(x.astype(BF16), y.astype(BF16)) for x, y in gather(*arrived_refs)]
    stacked = operand(blocks)
    store(two_products(matrix_ref, slice(0, stacked.shape[0]), stacked), own_ref, new_ref)


def on_odd_layer():
    return lax.axis_index("layer") % 2 == 1


def odd_kernel(mask_ref, matrix_ref, own_ref, all_ref, even_ref, odd_ref, new_ref, new_even_ref, new_odd_ref):
    @pl.when(on_odd_layer())
    def _():
        second_tick(matrix_ref, own_ref, (all_ref, even_ref, odd_ref), new_ref)

    @pl.when(jnp.logical_not(on_odd_layer()))
    def _():
        new_ref[...] = own_ref[...]

    choose(mask_ref, 0, new_ref, new_even_ref)
    choose(mask_ref, 1, new_ref, new_odd_ref)


def on_even_layer():
    layer = lax.axis_index("layer")
    return (layer % 2 == 0) & (layer > 0)


def even_kernel(mask_ref, matrix_ref, own_ref, known_ref, all_ref, even_ref, odd_ref, new_ref, new_even_ref, new_odd_ref):
    @pl.when(jnp.logical_not(on_even_layer()))
    def _():
        new_ref[...] = known_ref[...]

    @pl.when(on_even_layer())
    def _():
        second_tick(matrix_ref, own_ref, (all_ref, even_ref, odd_ref), new_ref)

    choose(mask_ref, 0, new_ref, new_even_ref)
    choose(mask_ref, 1, new_ref, new_odd_ref)


def own_kernel(matrix_ref, source_ref, trace_ref, own_ref):
    blocks = gather(trace_ref)
    depth = 2 * trace_ref.shape[2] * len(blocks)
    store(three_products(matrix_ref, slice(matrix_ref.shape[1] - depth, None), blocks), source_ref, own_ref)


def third_tick(matrix_ref, first, base_ref, refs, out_ref):
    blocks = gather(*refs)
    unit = 2 * base_ref.shape[2]
    columns = slice(first * unit, (first + len(blocks)) * unit)
    store(three_products(matrix_ref, columns, blocks), base_ref, out_ref)


def mate_kernel(matrix_ref, base_ref, pair_ref, out_ref):
    @pl.when(jnp.logical_not(on_odd_layer()))
    def _():
        out_ref[...] = base_ref[...]

    @pl.when(on_odd_layer())
    def _():
        third_tick(matrix_ref, 0, base_ref, (pair_ref.at[0],), out_ref)


def even_part_kernel(matrix_ref, base_ref, all_ref, even_ref, out_ref, final_hbm, sem):
    @pl.when(lax.axis_index("layer") == 0)
    def _():
        copy = pltpu.make_async_copy(base_ref, final_hbm, sem)
        copy.start()
        copy.wait()

    @pl.when(on_odd_layer())
    def _():
        out_ref[...] = base_ref[...]

    @pl.when(on_even_layer())
    def _():
        third_tick(matrix_ref, 0, base_ref, (all_ref, even_ref), out_ref)


def last_kernel(
    matrix_ref, base_ref, outer_odd_ref, inner_even_ref, inner_odd_ref, begun_hbm, final_hbm, out_ref, sem
):
    blocks = base_ref.shape[0]

    @pl.when(on_odd_layer())
    def _():
        third_tick(matrix_ref, blocks, base_ref, (inner_even_ref, inner_odd_ref), out_ref)

    @pl.when(on_even_layer())
    def _():
        third_tick(matrix_ref, blocks + inner_even_ref.shape[0], base_ref, (outer_odd_ref,), out_ref)

    @pl.when(lax.axis_index("layer") > 0)
    def _():
        copy = pltpu.make_async_copy(out_ref, final_hbm, sem)
        copy.start()
        copy.wait()


def call(kernel, ins, outs, flops, scratch=(), in_hbm=False, moved=None, last_in_hbm=False, last_out_hbm=False):
    if moved is None:
        moved = sum(x.size * x.dtype.itemsize for x in (*ins, *outs))
    vmem = pl.BlockSpec(memory_space=pltpu.VMEM)
    hbm = pl.BlockSpec(memory_space=pltpu.HBM)
    held = [in_hbm and not (x.ndim == 4 and x.dtype == F32) for x in ins]
    if last_in_hbm:
        held[-1] = True
    ins = [pltpu.with_memory_space_constraint(x, pltpu.HBM) if h else x for x, h in zip(ins, held)]
    out_specs = [vmem] * len(outs)
    if last_out_hbm:
        out_specs[-1] = hbm
        outs = (*outs[:-1], pltpu.HBM(outs[-1].shape, outs[-1].dtype))
    return pl.pallas_call(
        kernel,
        out_shape=outs,
        in_specs=[hbm if h else vmem for h in held],
        out_specs=out_specs,
        scratch_shapes=scratch,
        input_output_aliases={len(ins) - 1: len(outs) - 1} if last_in_hbm else {},
        compiler_params=pltpu.CompilerParams(vmem_limit_bytes=LIMIT),
        cost_estimate=pl.CostEstimate(flops=flops, bytes_accessed=moved, transcendentals=0),
    )(*ins)


def per_device(sources, operator_tiles, tile_rows, tile_cols, send_blocks):
    source = sources[0]
    tiles = operator_tiles[0]
    rows = tile_rows.reshape(-1)
    cols = tile_cols.reshape(-1)
    send = send_blocks.reshape(-1)
    blocks, _, width, shots = source.shape
    listed = send_blocks.shape[2]
    extended = 2 * blocks + 2 * listed
    shape = jax.ShapeDtypeStruct
    trace = shape(source.shape, F32)
    part = shape((listed, 2, width, shots), F32)
    matrix = shape((2 * blocks * width, extended * 2 * width), BF16)
    mask = shape((2, listed, blocks, 8, shots), F32)
    flops = 2 * blocks * width * extended * 2 * width * 2 * shots

    send_copy = pltpu.SMEM(send.shape, send.dtype)
    source_copy = pltpu.VMEM(source.shape, source.dtype)
    whole, even, odd = call(
        widen_kernel,
        (send, source),
        (trace, part, part),
        10**11,
        [send_copy, source_copy, pltpu.SemaphoreType.DMA((2,))],
        in_hbm=True,
        moved=10**8,
    )
    mate = permute(whole, inward, same)
    (later,) = call(after_kernel, (mate, odd), (part,), 0)
    whole = permute(whole, outward, same)
    from_odd = permute(even, outward, even_pair), permute(later, outward, odd_pair)
    from_even = permute(even, inward, even_pair), permute(odd, inward, odd_pair)
    matrix, own, mask = call(
        prepare_kernel,
        (rows, cols, send, source, tiles),
        (matrix, trace, mask),
        flops,
        [
            pltpu.SMEM(rows.shape, rows.dtype),
            pltpu.SMEM(cols.shape, cols.dtype),
            send_copy,
            source_copy,
            pltpu.VMEM((blocks * extended, width, 2 * width), F32),
            pltpu.SemaphoreType.DMA((4,)),
        ],
        in_hbm=True,
    )
    second, even, odd = call(odd_kernel, (mask, matrix, own, mate, *from_even), (trace, part, part), flops)
    early = permute(second, outward, same), permute(even, outward, even_pair), permute(odd, outward, odd_pair)
    traces, even, odd = call(
        even_kernel, (mask, matrix, own, second, whole, *from_odd), (trace, part, part), flops)
    late_even = permute(even, inward, even_pair)
    late_odd = permute(odd, inward, odd_pair)
    pair = with_mate(traces)
    (own,) = call(own_kernel, (matrix, source, traces), (trace,), flops)
    (own,) = call(mate_kernel, (matrix, own, pair), (trace,), flops)
    own, begun = call(
        even_part_kernel,
        (matrix, own, *early[:2]),
        (trace, trace),
        10**11,
        [pltpu.SemaphoreType.DMA],
        moved=10**9,
        last_out_hbm=True,
    )
    (out,) = call(
        last_kernel,
        (matrix, own, early[2], late_even, late_odd, begun),
        (trace,),
        flops,
        [pltpu.VMEM(trace.shape, F32), pltpu.SemaphoreType.DMA],
        last_in_hbm=True,
        last_out_hbm=True,
    )
    return out[None]


def solution(mesh):
    placed = (
        P("layer", "plane", None, None, None),
        P("layer", "plane", None, None, None),
        P("layer", "plane"),
        P("layer", "plane"),
        P("plane", None, None),
    )
    return jax.shard_map(
        per_device,
        mesh=mesh,
        in_specs=placed,
        out_specs=P("layer", "plane", None, None, None),
        check_vma=False,
    )
```

```python
import jax
import jax.numpy as jnp
from jax import lax
from jax.experimental import pallas as pl
from jax.experimental.pallas import tpu as pltpu
from jax.sharding import PartitionSpec as P

F32 = jnp.float32
BF16 = jnp.bfloat16
LIMIT = 40 * 1024 * 1024
LONG = 10**11


def even_pair(p, planes):
    q = p + 1 if p % 2 == 0 else p - 1
    return q if q < planes else p


def odd_pair(p, planes):
    q = p - 1 if p % 2 == 0 else p + 1
    return q if 0 <= q < planes else p


def same(p, planes):
    return p


def outward(l, p, layers, planes, partner):
    return (l + 1) % layers, partner(p, planes) if l % 2 == 1 and l + 1 < layers else p


def inward(l, p, layers, planes, partner):
    if l % 2 == 1:
        return l - 1, p
    return (l + 1, partner(p, planes)) if l + 1 < layers else (l, p)


def permute(block, way, partner):
    layers = lax.axis_size("layer")
    planes = lax.axis_size("plane")
    route = []
    for l in range(layers):
        for p in range(planes):
            to_layer, to_plane = way(l, p, layers, planes, partner)
            route.append((l * planes + p, to_layer * planes + to_plane))
    return lax.ppermute(block, ("layer", "plane"), route)


def with_mate(block):
    layers = lax.axis_size("layer")
    if layers % 2:
        return permute(block, inward, same)[None]
    groups = [[l, l + 1] for l in range(0, layers, 2)]
    return lax.all_gather(block, "layer", axis_index_groups=groups)


def split(value):
    high = value.astype(BF16)
    return high, (value - high.astype(F32)).astype(BF16)


def operand(blocks):
    rows = []
    for real, imag in blocks:
        rows.append(jnp.concatenate([real, imag], axis=1))
        rows.append(jnp.concatenate([-imag, real], axis=1))
    return jnp.concatenate(rows, axis=0)


def product(a, b):
    return jnp.dot(a, b, preferred_element_type=F32)


def two_products(matrix_ref, columns, operand_value):
    both = product(matrix_ref[:, columns], operand_value)
    half = both.shape[0] // 2
    return both[:half] + both[half:]


def three_products(matrix_ref, columns, blocks):
    halves = [(split(x), split(y)) for x, y in blocks]
    high = operand([(x[0], y[0]) for x, y in halves])
    low = operand([(x[1], y[1]) for x, y in halves])
    half = matrix_ref.shape[0] // 2
    return two_products(matrix_ref, columns, high) + product(matrix_ref[:half, columns], low)


def store(result, base_ref, out_ref):
    blocks, _, width, shots = base_ref.shape
    for b in range(blocks):
        for part in range(2):
            out_ref[b, part] = (
                result[b * width : (b + 1) * width, part * shots : (part + 1) * shots]
                + base_ref[b, part].astype(F32)
            )


def fetch(pairs, sems):
    copies = [pltpu.make_async_copy(a, b, sems.at[i]) for i, (a, b) in enumerate(pairs)]
    for copy in copies:
        copy.start()
    return copies


def widen_kernel(send_hbm, source_hbm, all_ref, even_ref, odd_ref, send_ref, source_ref, sems):
    copies = fetch([(source_hbm, source_ref), (send_hbm, send_ref)], sems)
    is_odd = lax.axis_index("plane") % 2
    listed = even_ref.shape[0]
    copies[0].wait()
    all_ref[...] = source_ref[...].astype(F32)
    copies[1].wait()
    for k in range(listed):
        even_ref[k] = source_ref[send_ref[(1 - is_odd) * listed + k]].astype(F32)
        odd_ref[k] = source_ref[send_ref[is_odd * listed + k]].astype(F32)


def after_kernel(first_ref, payload_ref, passed_ref):
    passed_ref[...] = payload_ref[...]


def prepare_kernel(
    rows_hbm, cols_hbm, send_hbm, source_hbm, tiles_ref,
    matrix_ref, own_ref, mask_ref,
    rows_ref, cols_ref, send_ref, source_ref, total, sems,
):
    tile_count, _, width, _ = tiles_ref.shape
    blocks_here = source_ref.shape[0]
    extended = total.shape[0] // blocks_here
    listed = (extended - 2 * blocks_here) // 2
    small = [(rows_hbm, rows_ref), (cols_hbm, cols_ref), (send_hbm, send_ref)]
    copies = fetch(small + [(source_hbm, source_ref)], sems)
    layer = lax.axis_index("layer")
    plane = lax.axis_index("plane")
    planes = lax.axis_size("plane")
    is_odd = plane % 2
    total[...] = jnp.zeros_like(total)

    def add(t, carry):
        col = cols_ref[t]
        is_lower = (col >= blocks_here) & (col < blocks_here + listed)
        is_upper = (col >= blocks_here + listed) & (col < blocks_here + 2 * listed)
        place = jnp.where(is_lower & (is_odd == 0), col + listed, col)
        place = jnp.where(is_upper & (is_odd == 0), col - listed, place)
        slot = rows_ref[t] * extended + place
        total[slot, :, :width] += tiles_ref[t, 0]
        total[slot, :, width:] += tiles_ref[t, 1]
        return carry

    for copy in copies[:3]:
        copy.wait()
    for k in range(listed):
        to_even = send_ref[(1 - is_odd) * listed + k]
        to_odd = send_ref[is_odd * listed + k]
        for b in range(blocks_here):
            for kind, chosen in enumerate((to_even, to_odd)):
                mask_ref[kind, k, b] = jnp.full(mask_ref.shape[3:], jnp.where(chosen == b, 1.0, 0.0), F32)
    lax.fori_loop(0, tile_count, add, 0, unroll=8)
    has_layer = layer > 0
    has_next = plane + 1 < planes
    has_even = has_layer & ((is_odd == 1) | has_next)
    has_odd = has_layer & jnp.where(is_odd == 1, has_next, plane > 0)
    height = blocks_here * width
    for c in range(extended):
        keep = None
        if c < blocks_here:
            keep = has_layer
        elif c < blocks_here + listed:
            keep = has_even
        elif c < blocks_here + 2 * listed:
            keep = has_odd
        for r in range(blocks_here):
            value = total[r * extended + c]
            if keep is not None:
                value = jnp.where(keep, value, 0.0)
            high, low = split(value)
            here = slice(c * 2 * width, (c + 1) * 2 * width)
            matrix_ref[r * width : (r + 1) * width, here] = high
            matrix_ref[height + r * width : height + (r + 1) * width, here] = low
    copies[-1].wait()
    own = operand([(source_ref[b, 0], source_ref[b, 1]) for b in range(blocks_here)])
    columns = slice((extended - blocks_here) * 2 * width, None)
    store(two_products(matrix_ref, columns, own), source_ref, own_ref)


def gather(*refs):
    return [(ref[b, 0], ref[b, 1]) for ref in refs for b in range(ref.shape[0])]


def choose(mask_ref, kind, new_ref, out_ref):
    count, _, width, shots = new_ref.shape
    rows = mask_ref.shape[3]
    for k in range(out_ref.shape[0]):
        chosen = jnp.zeros((2, width // rows, rows, shots), F32)
        for b in range(count):
            block = new_ref[b].reshape(chosen.shape)
            chosen = jnp.where(mask_ref[kind, k, b][None, None] > 0.5, block, chosen)
        out_ref[k] = chosen.reshape(2, width, shots)


def second_tick(matrix_ref, own_ref, arrived_refs, new_ref):
    blocks = [(x.astype(BF16), y.astype(BF16)) for x, y in gather(*arrived_refs)]
    stacked = operand(blocks)
    store(two_products(matrix_ref, slice(0, stacked.shape[0]), stacked), own_ref, new_ref)


def on_odd_layer():
    return lax.axis_index("layer") % 2 == 1


def odd_kernel(mask_ref, matrix_ref, own_ref, all_ref, even_ref, odd_ref, new_ref, new_even_ref, new_odd_ref):
    @pl.when(on_odd_layer())
    def _():
        second_tick(matrix_ref, own_ref, (all_ref, even_ref, odd_ref), new_ref)

    @pl.when(jnp.logical_not(on_odd_layer()))
    def _():
        new_ref[...] = own_ref[...]

    choose(mask_ref, 0, new_ref, new_even_ref)
    choose(mask_ref, 1, new_ref, new_odd_ref)


def on_even_layer():
    layer = lax.axis_index("layer")
    return (layer % 2 == 0) & (layer > 0)


def even_kernel(mask_ref, matrix_ref, own_ref, known_ref, all_ref, even_ref, odd_ref, new_ref, new_even_ref, new_odd_ref):
    @pl.when(jnp.logical_not(on_even_layer()))
    def _():
        new_ref[...] = known_ref[...]

    @pl.when(on_even_layer())
    def _():
        second_tick(matrix_ref, own_ref, (all_ref, even_ref, odd_ref), new_ref)

    choose(mask_ref, 0, new_ref, new_even_ref)
    choose(mask_ref, 1, new_ref, new_odd_ref)


def third_tick(matrix_ref, first, base_ref, refs, out_ref):
    blocks = gather(*refs)
    unit = 2 * base_ref.shape[2]
    columns = slice(first * unit, (first + len(blocks)) * unit)
    store(three_products(matrix_ref, columns, blocks), base_ref, out_ref)


def first_own_column(matrix_ref, trace_ref):
    blocks, _, width, _ = trace_ref.shape
    return matrix_ref.shape[1] // (2 * width) - blocks


def odd_own_kernel(matrix_ref, source_ref, trace_ref, payload_ref, out_ref, passed_ref):
    passed_ref[...] = payload_ref[...]

    @pl.when(on_odd_layer())
    def _():
        third_tick(matrix_ref, first_own_column(matrix_ref, trace_ref), source_ref, (trace_ref,), out_ref)

    @pl.when(jnp.logical_not(on_odd_layer()))
    def _():
        out_ref[...] = source_ref[...].astype(F32)


def pair_kernel(matrix_ref, base_ref, trace_ref, pair_ref, out_ref):
    @pl.when(on_odd_layer())
    def _():
        third_tick(matrix_ref, 0, base_ref, (pair_ref.at[0],), out_ref)

    @pl.when(jnp.logical_not(on_odd_layer()))
    def _():
        third_tick(matrix_ref, first_own_column(matrix_ref, trace_ref), base_ref, (trace_ref,), out_ref)


def even_part_kernel(matrix_ref, base_ref, all_ref, even_ref, out_ref, final_hbm, sem):
    @pl.when(lax.axis_index("layer") == 0)
    def _():
        copy = pltpu.make_async_copy(base_ref, final_hbm, sem)
        copy.start()
        copy.wait()

    @pl.when(on_odd_layer())
    def _():
        out_ref[...] = base_ref[...]

    @pl.when(on_even_layer())
    def _():
        third_tick(matrix_ref, 0, base_ref, (all_ref, even_ref), out_ref)


def last_kernel(
    matrix_ref, base_ref, outer_odd_ref, inner_even_ref, inner_odd_ref, begun_hbm, final_hbm, out_ref, sem
):
    blocks = base_ref.shape[0]

    @pl.when(on_odd_layer())
    def _():
        third_tick(matrix_ref, blocks, base_ref, (inner_even_ref, inner_odd_ref), out_ref)

    @pl.when(on_even_layer())
    def _():
        third_tick(matrix_ref, blocks + inner_even_ref.shape[0], base_ref, (outer_odd_ref,), out_ref)

    @pl.when(lax.axis_index("layer") > 0)
    def _():
        copy = pltpu.make_async_copy(out_ref, final_hbm, sem)
        copy.start()
        copy.wait()


def call(kernel, ins, outs, flops, scratch=(), in_hbm=False, moved=None, last_in_hbm=False, last_out_hbm=False):
    if moved is None:
        moved = sum(x.size * x.dtype.itemsize for x in (*ins, *outs))
    vmem = pl.BlockSpec(memory_space=pltpu.VMEM)
    hbm = pl.BlockSpec(memory_space=pltpu.HBM)
    held = [in_hbm and not (x.ndim == 4 and x.dtype == F32) for x in ins]
    if last_in_hbm:
        held[-1] = True
    ins = [pltpu.with_memory_space_constraint(x, pltpu.HBM) if h else x for x, h in zip(ins, held)]
    out_specs = [vmem] * len(outs)
    if last_out_hbm:
        out_specs[-1] = hbm
        outs = (*outs[:-1], pltpu.HBM(outs[-1].shape, outs[-1].dtype))
    return pl.pallas_call(
        kernel,
        out_shape=outs,
        in_specs=[hbm if h else vmem for h in held],
        out_specs=out_specs,
        scratch_shapes=scratch,
        input_output_aliases={len(ins) - 1: len(outs) - 1} if last_in_hbm else {},
        compiler_params=pltpu.CompilerParams(vmem_limit_bytes=LIMIT),
        cost_estimate=pl.CostEstimate(flops=flops, bytes_accessed=moved, transcendentals=0),
    )(*ins)


def per_device(sources, operator_tiles, tile_rows, tile_cols, send_blocks):
    source = sources[0]
    tiles = operator_tiles[0]
    rows = tile_rows.reshape(-1)
    cols = tile_cols.reshape(-1)
    send = send_blocks.reshape(-1)
    blocks, _, width, shots = source.shape
    listed = send_blocks.shape[2]
    extended = 2 * blocks + 2 * listed
    shape = jax.ShapeDtypeStruct
    trace = shape(source.shape, F32)
    part = shape((listed, 2, width, shots), F32)
    matrix = shape((2 * blocks * width, extended * 2 * width), BF16)
    mask = shape((2, listed, blocks, 8, shots), F32)
    flops = 2 * blocks * width * extended * 2 * width * 2 * shots

    send_copy = pltpu.SMEM(send.shape, send.dtype)
    source_copy = pltpu.VMEM(source.shape, source.dtype)
    whole, even, odd = call(
        widen_kernel,
        (send, source),
        (trace, part, part),
        LONG,
        [send_copy, source_copy, pltpu.SemaphoreType.DMA((2,))],
        in_hbm=True,
        moved=10**8,
    )
    mate = permute(whole, inward, same)
    (later,) = call(after_kernel, (mate, odd), (part,), 0)
    whole = permute(whole, outward, same)
    from_odd = permute(even, outward, even_pair), permute(later, outward, odd_pair)
    from_even = permute(even, inward, even_pair), permute(odd, inward, odd_pair)
    matrix, own, mask = call(
        prepare_kernel,
        (rows, cols, send, source, tiles),
        (matrix, trace, mask),
        flops,
        [
            pltpu.SMEM(rows.shape, rows.dtype),
            pltpu.SMEM(cols.shape, cols.dtype),
            send_copy,
            source_copy,
            pltpu.VMEM((blocks * extended, width, 2 * width), F32),
            pltpu.SemaphoreType.DMA((4,)),
        ],
        in_hbm=True,
    )
    second, even, odd = call(odd_kernel, (mask, matrix, own, mate, *from_even), (trace, part, part), flops)
    third, odd = call(odd_own_kernel, (matrix, source, second, odd), (trace, part), flops)
    early = permute(second, outward, same), permute(even, outward, even_pair), permute(odd, outward, odd_pair)
    traces, even, odd = call(
        even_kernel, (mask, matrix, own, second, whole, *from_odd), (trace, part, part), flops
    )
    late_even = permute(even, inward, even_pair)
    late_odd = permute(odd, inward, odd_pair)
    pair = with_mate(traces)
    (own,) = call(pair_kernel, (matrix, third, traces, pair), (trace,), flops)
    own, begun = call(
        even_part_kernel,
        (matrix, own, *early[:2]),
        (trace, trace),
        LONG,
        [pltpu.SemaphoreType.DMA],
        moved=10**9,
        last_out_hbm=True,
    )
    (out,) = call(
        last_kernel,
        (matrix, own, early[2], late_even, late_odd, begun),
        (trace,),
        flops,
        [pltpu.VMEM(trace.shape, F32), pltpu.SemaphoreType.DMA],
        last_in_hbm=True,
        last_out_hbm=True,
    )
    return out[None]


def solution(mesh):
    placed = (
        P("layer", "plane", None, None, None),
        P("layer", "plane", None, None, None),
        P("layer", "plane"),
        P("layer", "plane"),
        P("plane", None, None),
    )
    return jax.shard_map(
        per_device,
        mesh=mesh,
        in_specs=placed,
        out_specs=P("layer", "plane", None, None, None),
        check_vma=False,
    )
```

```python
import jax
import jax.numpy as jnp
from jax import lax
from jax.experimental import pallas as pl
from jax.experimental.pallas import tpu as pltpu
from jax.sharding import PartitionSpec as P

F32 = jnp.float32
BF16 = jnp.bfloat16
LIMIT = 40 * 1024 * 1024
LONG = 10**11


def even_pair(p, planes):
    q = p + 1 if p % 2 == 0 else p - 1
    return q if q < planes else p


def odd_pair(p, planes):
    q = p - 1 if p % 2 == 0 else p + 1
    return q if 0 <= q < planes else p


def same(p, planes):
    return p


def outward(l, p, layers, planes, partner):
    return (l + 1) % layers, partner(p, planes) if l % 2 == 1 and l + 1 < layers else p


def inward(l, p, layers, planes, partner):
    if l % 2 == 1:
        return l - 1, p
    return (l + 1, partner(p, planes)) if l + 1 < layers else (l, p)


def permute(block, way, partner):
    layers = lax.axis_size("layer")
    planes = lax.axis_size("plane")
    route = []
    for l in range(layers):
        for p in range(planes):
            to_layer, to_plane = way(l, p, layers, planes, partner)
            route.append((l * planes + p, to_layer * planes + to_plane))
    return lax.ppermute(block, ("layer", "plane"), route)


def with_mate(block):
    layers = lax.axis_size("layer")
    if layers % 2:
        return permute(block, inward, same)[None]
    groups = [[l, l + 1] for l in range(0, layers, 2)]
    return lax.all_gather(block, "layer", axis_index_groups=groups)


def split(value):
    high = value.astype(BF16)
    return high, (value - high.astype(F32)).astype(BF16)


def operand(blocks):
    rows = []
    for real, imag in blocks:
        rows.append(jnp.concatenate([real, imag], axis=1))
        rows.append(jnp.concatenate([-imag, real], axis=1))
    return jnp.concatenate(rows, axis=0)


def product(a, b):
    return jnp.dot(a, b, preferred_element_type=F32)


def two_products(matrix_ref, columns, operand_value):
    both = product(matrix_ref[:, columns], operand_value)
    half = both.shape[0] // 2
    return both[:half] + both[half:]


def three_products(matrix_ref, columns, blocks):
    halves = [(split(x), split(y)) for x, y in blocks]
    high = operand([(x[0], y[0]) for x, y in halves])
    low = operand([(x[1], y[1]) for x, y in halves])
    half = matrix_ref.shape[0] // 2
    return two_products(matrix_ref, columns, high) + product(matrix_ref[:half, columns], low)


def store(result, base_ref, out_ref):
    blocks, _, width, shots = base_ref.shape
    for b in range(blocks):
        for part in range(2):
            out_ref[b, part] = (
                result[b * width : (b + 1) * width, part * shots : (part + 1) * shots]
                + base_ref[b, part].astype(F32)
            )


def fetch(pairs, sems):
    copies = [pltpu.make_async_copy(a, b, sems.at[i]) for i, (a, b) in enumerate(pairs)]
    for copy in copies:
        copy.start()
    return copies


def widen_kernel(send_hbm, source_hbm, all_ref, even_ref, odd_ref, send_ref, source_ref, sems):
    copies = fetch([(source_hbm, source_ref), (send_hbm, send_ref)], sems)
    is_odd = lax.axis_index("plane") % 2
    listed = even_ref.shape[0]
    copies[0].wait()
    all_ref[...] = source_ref[...].astype(F32)
    copies[1].wait()
    for k in range(listed):
        even_ref[k] = source_ref[send_ref[(1 - is_odd) * listed + k]].astype(F32)
        odd_ref[k] = source_ref[send_ref[is_odd * listed + k]].astype(F32)


def after_kernel(first_ref, payload_ref, passed_ref):
    passed_ref[...] = payload_ref[...]


def prepare_kernel(
    rows_hbm, cols_hbm, send_hbm, source_hbm, tiles_ref,
    matrix_ref, own_ref, mask_ref,
    rows_ref, cols_ref, send_ref, source_ref, total, sems,
):
    tile_count, _, width, _ = tiles_ref.shape
    blocks_here = source_ref.shape[0]
    extended = total.shape[0] // blocks_here
    listed = (extended - 2 * blocks_here) // 2
    small = [(rows_hbm, rows_ref), (cols_hbm, cols_ref), (send_hbm, send_ref)]
    copies = fetch(small + [(source_hbm, source_ref)], sems)
    layer = lax.axis_index("layer")
    plane = lax.axis_index("plane")
    planes = lax.axis_size("plane")
    is_odd = plane % 2
    total[...] = jnp.zeros_like(total)

    def add(t, carry):
        col = cols_ref[t]
        is_lower = (col >= blocks_here) & (col < blocks_here + listed)
        is_upper = (col >= blocks_here + listed) & (col < blocks_here + 2 * listed)
        place = jnp.where(is_lower & (is_odd == 0), col + listed, col)
        place = jnp.where(is_upper & (is_odd == 0), col - listed, place)
        slot = rows_ref[t] * extended + place
        total[slot, :, :width] += tiles_ref[t, 0]
        total[slot, :, width:] += tiles_ref[t, 1]
        return carry

    for copy in copies[:3]:
        copy.wait()
    for k in range(listed):
        to_even = send_ref[(1 - is_odd) * listed + k]
        to_odd = send_ref[is_odd * listed + k]
        for b in range(blocks_here):
            for kind, chosen in enumerate((to_even, to_odd)):
                mask_ref[kind, k, b] = jnp.full(mask_ref.shape[3:], jnp.where(chosen == b, 1.0, 0.0), F32)
    lax.fori_loop(0, tile_count, add, 0, unroll=8)
    has_layer = layer > 0
    has_next = plane + 1 < planes
    has_even = has_layer & ((is_odd == 1) | has_next)
    has_odd = has_layer & jnp.where(is_odd == 1, has_next, plane > 0)
    height = blocks_here * width
    for c in range(extended):
        keep = None
        if c < blocks_here:
            keep = has_layer
        elif c < blocks_here + listed:
            keep = has_even
        elif c < blocks_here + 2 * listed:
            keep = has_odd
        for r in range(blocks_here):
            value = total[r * extended + c]
            if keep is not None:
                value = jnp.where(keep, value, 0.0)
            high, low = split(value)
            here = slice(c * 2 * width, (c + 1) * 2 * width)
            matrix_ref[r * width : (r + 1) * width, here] = high
            matrix_ref[height + r * width : height + (r + 1) * width, here] = low
    copies[-1].wait()
    own = operand([(source_ref[b, 0], source_ref[b, 1]) for b in range(blocks_here)])
    columns = slice((extended - blocks_here) * 2 * width, None)
    store(two_products(matrix_ref, columns, own), source_ref, own_ref)


def gather(*refs):
    return [(ref[b, 0], ref[b, 1]) for ref in refs for b in range(ref.shape[0])]


def choose(mask_ref, kind, new_ref, out_ref):
    count, _, width, shots = new_ref.shape
    rows = mask_ref.shape[3]
    for k in range(out_ref.shape[0]):
        chosen = jnp.zeros((2, width // rows, rows, shots), F32)
        for b in range(count):
            block = new_ref[b].reshape(chosen.shape)
            chosen = jnp.where(mask_ref[kind, k, b][None, None] > 0.5, block, chosen)
        out_ref[k] = chosen.reshape(2, width, shots)


def second_tick(matrix_ref, own_ref, arrived_refs, new_ref):
    blocks = [(x.astype(BF16), y.astype(BF16)) for x, y in gather(*arrived_refs)]
    stacked = operand(blocks)
    store(two_products(matrix_ref, slice(0, stacked.shape[0]), stacked), own_ref, new_ref)


def on_odd_layer():
    return lax.axis_index("layer") % 2 == 1


def odd_kernel(mask_ref, matrix_ref, own_ref, all_ref, even_ref, odd_ref, new_ref, new_even_ref, new_odd_ref):
    @pl.when(on_odd_layer())
    def _():
        second_tick(matrix_ref, own_ref, (all_ref, even_ref, odd_ref), new_ref)

    @pl.when(jnp.logical_not(on_odd_layer()))
    def _():
        new_ref[...] = own_ref[...]

    choose(mask_ref, 0, new_ref, new_even_ref)
    choose(mask_ref, 1, new_ref, new_odd_ref)


def on_even_layer():
    layer = lax.axis_index("layer")
    return (layer % 2 == 0) & (layer > 0)


def even_kernel(mask_ref, matrix_ref, own_ref, known_ref, all_ref, even_ref, odd_ref, new_ref, new_even_ref, new_odd_ref):
    @pl.when(jnp.logical_not(on_even_layer()))
    def _():
        new_ref[...] = known_ref[...]

    @pl.when(on_even_layer())
    def _():
        second_tick(matrix_ref, own_ref, (all_ref, even_ref, odd_ref), new_ref)

    choose(mask_ref, 0, new_ref, new_even_ref)
    choose(mask_ref, 1, new_ref, new_odd_ref)


def third_tick(matrix_ref, first, base_ref, refs, out_ref):
    blocks = gather(*refs)
    unit = 2 * base_ref.shape[2]
    columns = slice(first * unit, (first + len(blocks)) * unit)
    store(three_products(matrix_ref, columns, blocks), base_ref, out_ref)


def first_own_column(matrix_ref, trace_ref):
    blocks, _, width, _ = trace_ref.shape
    return matrix_ref.shape[1] // (2 * width) - blocks


def odd_own_kernel(matrix_ref, source_ref, trace_ref, payload_ref, out_ref, passed_ref):
    passed_ref[...] = payload_ref[...]

    @pl.when(on_odd_layer())
    def _():
        third_tick(matrix_ref, first_own_column(matrix_ref, trace_ref), source_ref, (trace_ref,), out_ref)

    @pl.when(jnp.logical_not(on_odd_layer()))
    def _():
        out_ref[...] = source_ref[...].astype(F32)


def pair_kernel(matrix_ref, base_ref, trace_ref, pair_ref, out_ref):
    @pl.when(on_odd_layer())
    def _():
        third_tick(matrix_ref, 0, base_ref, (pair_ref.at[0],), out_ref)

    @pl.when(jnp.logical_not(on_odd_layer()))
    def _():
        third_tick(matrix_ref, first_own_column(matrix_ref, trace_ref), base_ref, (trace_ref,), out_ref)


def even_part_kernel(matrix_ref, base_ref, all_ref, even_ref, out_ref, final_hbm, sem):
    @pl.when(lax.axis_index("layer") == 0)
    def _():
        copy = pltpu.make_async_copy(base_ref, final_hbm, sem)
        copy.start()
        copy.wait()

    @pl.when(on_odd_layer())
    def _():
        out_ref[...] = base_ref[...]

    @pl.when(on_even_layer())
    def _():
        third_tick(matrix_ref, 0, base_ref, (all_ref, even_ref), out_ref)


def last_kernel(
    matrix_ref, base_ref, outer_odd_ref, inner_even_ref, inner_odd_ref, begun_hbm, final_hbm, out_ref, sem
):
    blocks = base_ref.shape[0]

    @pl.when(on_odd_layer())
    def _():
        third_tick(matrix_ref, blocks, base_ref, (inner_even_ref, inner_odd_ref), out_ref)

    @pl.when(on_even_layer())
    def _():
        third_tick(matrix_ref, blocks + inner_even_ref.shape[0], base_ref, (outer_odd_ref,), out_ref)

    @pl.when(lax.axis_index("layer") > 0)
    def _():
        copy = pltpu.make_async_copy(out_ref, final_hbm, sem)
        copy.start()
        copy.wait()


def call(kernel, ins, outs, flops, scratch=(), in_hbm=False, moved=None, last_in_hbm=False, last_out_hbm=False):
    if moved is None:
        moved = sum(x.size * x.dtype.itemsize for x in (*ins, *outs))
    vmem = pl.BlockSpec(memory_space=pltpu.VMEM)
    hbm = pl.BlockSpec(memory_space=pltpu.HBM)
    held = [in_hbm and not (x.ndim == 4 and x.dtype == F32) for x in ins]
    if last_in_hbm:
        held[-1] = True
    ins = [pltpu.with_memory_space_constraint(x, pltpu.HBM) if h else x for x, h in zip(ins, held)]
    out_specs = [vmem] * len(outs)
    if last_out_hbm:
        out_specs[-1] = hbm
        outs = (*outs[:-1], pltpu.HBM(outs[-1].shape, outs[-1].dtype))
    return pl.pallas_call(
        kernel,
        out_shape=outs,
        in_specs=[hbm if h else vmem for h in held],
        out_specs=out_specs,
        scratch_shapes=scratch,
        input_output_aliases={len(ins) - 1: len(outs) - 1} if last_in_hbm else {},
        compiler_params=pltpu.CompilerParams(vmem_limit_bytes=LIMIT),
        cost_estimate=pl.CostEstimate(flops=flops, bytes_accessed=moved, transcendentals=0),
    )(*ins)


def per_device(sources, operator_tiles, tile_rows, tile_cols, send_blocks):
    source = sources[0]
    tiles = operator_tiles[0]
    rows = tile_rows.reshape(-1)
    cols = tile_cols.reshape(-1)
    send = send_blocks.reshape(-1)
    blocks, _, width, shots = source.shape
    listed = send_blocks.shape[2]
    extended = 2 * blocks + 2 * listed
    shape = jax.ShapeDtypeStruct
    trace = shape(source.shape, F32)
    part = shape((listed, 2, width, shots), F32)
    matrix = shape((2 * blocks * width, extended * 2 * width), BF16)
    mask = shape((2, listed, blocks, 8, shots), F32)
    flops = 2 * blocks * width * extended * 2 * width * 2 * shots

    send_copy = pltpu.SMEM(send.shape, send.dtype)
    source_copy = pltpu.VMEM(source.shape, source.dtype)
    whole, even, odd = call(
        widen_kernel,
        (send, source),
        (trace, part, part),
        LONG,
        [send_copy, source_copy, pltpu.SemaphoreType.DMA((2,))],
        in_hbm=True,
        moved=10**8,
    )
    mate = permute(whole, inward, same)
    (later,) = call(after_kernel, (mate, even), (part,), 0)
    whole = permute(whole, outward, same)
    from_odd = permute(later, outward, even_pair), permute(odd, outward, odd_pair)
    from_even = permute(even, inward, even_pair), permute(odd, inward, odd_pair)
    matrix, own, mask = call(
        prepare_kernel,
        (rows, cols, send, source, tiles),
        (matrix, trace, mask),
        flops,
        [
            pltpu.SMEM(rows.shape, rows.dtype),
            pltpu.SMEM(cols.shape, cols.dtype),
            send_copy,
            source_copy,
            pltpu.VMEM((blocks * extended, width, 2 * width), F32),
            pltpu.SemaphoreType.DMA((4,)),
        ],
        in_hbm=True,
    )
    second, even, odd = call(odd_kernel, (mask, matrix, own, mate, *from_even), (trace, part, part), flops)
    third, odd = call(odd_own_kernel, (matrix, source, second, odd), (trace, part), flops)
    early = permute(second, outward, same), permute(even, outward, even_pair), permute(odd, outward, odd_pair)
    traces, even, odd = call(
        even_kernel, (mask, matrix, own, second, whole, *from_odd), (trace, part, part), flops
    )
    late_even = permute(even, inward, even_pair)
    late_odd = permute(odd, inward, odd_pair)
    pair = with_mate(traces)
    (own,) = call(pair_kernel, (matrix, third, traces, pair), (trace,), flops)
    own, begun = call(
        even_part_kernel,
        (matrix, own, *early[:2]),
        (trace, trace),
        LONG,
        [pltpu.SemaphoreType.DMA],
        moved=10**9,
        last_out_hbm=True,
    )
    (out,) = call(
        last_kernel,
        (matrix, own, early[2], late_even, late_odd, begun),
        (trace,),
        flops,
        [pltpu.VMEM(trace.shape, F32), pltpu.SemaphoreType.DMA],
        last_in_hbm=True,
        last_out_hbm=True,
    )
    return out[None]


def solution(mesh):
    placed = (
        P("layer", "plane", None, None, None),
        P("layer", "plane", None, None, None),
        P("layer", "plane"),
        P("layer", "plane"),
        P("plane", None, None),
    )
    return jax.shard_map(
        per_device,
        mesh=mesh,
        in_specs=placed,
        out_specs=P("layer", "plane", None, None, None),
        check_vma=False,
    )
```

```python
import jax
import jax.numpy as jnp
from jax import lax
from jax.experimental import pallas as pl
from jax.experimental.pallas import tpu as pltpu
from jax.sharding import PartitionSpec as P

F32 = jnp.float32
BF16 = jnp.bfloat16
LIMIT = 40 * 1024 * 1024


def even_pair(p, planes):
    q = p + 1 if p % 2 == 0 else p - 1
    return q if q < planes else p


def odd_pair(p, planes):
    q = p - 1 if p % 2 == 0 else p + 1
    return q if 0 <= q < planes else p


def same(p, planes):
    return p


def outward(l, p, layers, planes, partner):
    return (l + 1) % layers, partner(p, planes) if l % 2 == 1 and l + 1 < layers else p


def inward(l, p, layers, planes, partner):
    if l % 2 == 1:
        return l - 1, p
    return (l + 1, partner(p, planes)) if l + 1 < layers else (l, p)


def permute(block, way, partner):
    layers = lax.axis_size("layer")
    planes = lax.axis_size("plane")
    route = []
    for l in range(layers):
        for p in range(planes):
            to_layer, to_plane = way(l, p, layers, planes, partner)
            route.append((l * planes + p, to_layer * planes + to_plane))
    return lax.ppermute(block, ("layer", "plane"), route)


def onward(l, p, layers, planes, partner):
    return (l + 1) % layers, p


def with_mate(block):
    layers = lax.axis_size("layer")
    if layers % 2:
        return permute(block, inward, same)[None]
    groups = [[l, l + 1] for l in range(0, layers, 2)]
    return lax.all_gather(block, "layer", axis_index_groups=groups)


def split(value):
    high = value.astype(BF16)
    return high, (value - high.astype(F32)).astype(BF16)


def operand(blocks):
    rows = []
    for real, imag in blocks:
        rows.append(jnp.concatenate([real, imag], axis=1))
        rows.append(jnp.concatenate([-imag, real], axis=1))
    return jnp.concatenate(rows, axis=0)


def product(a, b):
    return jnp.dot(a, b, preferred_element_type=F32)


def two_products(matrix_ref, columns, operand_value):
    both = product(matrix_ref[:, columns], operand_value)
    half = both.shape[0] // 2
    return both[:half] + both[half:]


def three_products(matrix_ref, columns, blocks):
    halves = [(split(x), split(y)) for x, y in blocks]
    high = operand([(x[0], y[0]) for x, y in halves])
    low = operand([(x[1], y[1]) for x, y in halves])
    half = matrix_ref.shape[0] // 2
    return two_products(matrix_ref, columns, high) + product(matrix_ref[:half, columns], low)


def store(result, base_ref, out_ref):
    blocks, _, width, shots = base_ref.shape
    for b in range(blocks):
        for part in range(2):
            out_ref[b, part] = (
                result[b * width : (b + 1) * width, part * shots : (part + 1) * shots]
                + base_ref[b, part].astype(F32)
            )


def fetch(pairs, sems):
    copies = [pltpu.make_async_copy(a, b, sems.at[i]) for i, (a, b) in enumerate(pairs)]
    for copy in copies:
        copy.start()
    return copies


def widen_kernel(send_hbm, source_hbm, all_ref, even_ref, odd_ref, send_ref, source_ref, sems):
    copies = fetch([(source_hbm, source_ref), (send_hbm, send_ref)], sems)
    is_odd = lax.axis_index("plane") % 2
    listed = even_ref.shape[0]
    copies[0].wait()
    all_ref[...] = source_ref[...].astype(F32)
    copies[1].wait()
    for k in range(listed):
        even_ref[k] = source_ref[send_ref[(1 - is_odd) * listed + k]].astype(F32)
        odd_ref[k] = source_ref[send_ref[is_odd * listed + k]].astype(F32)


def after_kernel(first_ref, payload_ref, passed_ref):
    passed_ref[...] = payload_ref[...]


def prepare_kernel(
    rows_in, cols_in, send_in, source_ref, tiles_ref,
    matrix_ref, own_ref, mask_ref,
    rows_ref, cols_ref, send_ref, total, sems,
):
    tile_count, _, width, _ = tiles_ref.shape
    blocks_here = source_ref.shape[0]
    extended = total.shape[0] // blocks_here
    listed = (extended - 2 * blocks_here) // 2
    copies = fetch([(rows_in, rows_ref), (cols_in, cols_ref), (send_in, send_ref)], sems)
    layer = lax.axis_index("layer")
    plane = lax.axis_index("plane")
    planes = lax.axis_size("plane")
    is_odd = plane % 2
    total[...] = jnp.zeros_like(total)

    def add(t, carry):
        col = cols_ref[t]
        is_lower = (col >= blocks_here) & (col < blocks_here + listed)
        is_upper = (col >= blocks_here + listed) & (col < blocks_here + 2 * listed)
        place = jnp.where(is_lower & (is_odd == 0), col + listed, col)
        place = jnp.where(is_upper & (is_odd == 0), col - listed, place)
        slot = rows_ref[t] * extended + place
        total[slot, :, :width] += tiles_ref[t, 0]
        total[slot, :, width:] += tiles_ref[t, 1]
        return carry

    for copy in copies:
        copy.wait()
    for k in range(listed):
        to_even = send_ref[(1 - is_odd) * listed + k]
        to_odd = send_ref[is_odd * listed + k]
        for b in range(blocks_here):
            for kind, chosen in enumerate((to_even, to_odd)):
                mask_ref[kind, k, b] = jnp.full(mask_ref.shape[3:], jnp.where(chosen == b, 1.0, 0.0), F32)
    lax.fori_loop(0, tile_count, add, 0, unroll=8)
    has_layer = layer > 0
    has_next = plane + 1 < planes
    has_even = has_layer & ((is_odd == 1) | has_next)
    has_odd = has_layer & jnp.where(is_odd == 1, has_next, plane > 0)
    height = blocks_here * width
    for c in range(extended):
        keep = None
        if c < blocks_here:
            keep = has_layer
        elif c < blocks_here + listed:
            keep = has_even
        elif c < blocks_here + 2 * listed:
            keep = has_odd
        for r in range(blocks_here):
            value = total[r * extended + c]
            if keep is not None:
                value = jnp.where(keep, value, 0.0)
            high, low = split(value)
            here = slice(c * 2 * width, (c + 1) * 2 * width)
            matrix_ref[r * width : (r + 1) * width, here] = high
            matrix_ref[height + r * width : height + (r + 1) * width, here] = low
    own = operand([(source_ref[b, 0], source_ref[b, 1]) for b in range(blocks_here)])
    columns = slice((extended - blocks_here) * 2 * width, None)
    store(two_products(matrix_ref, columns, own), source_ref, own_ref)


def gather(*refs):
    return [(ref[b, 0], ref[b, 1]) for ref in refs for b in range(ref.shape[0])]


def choose(mask_ref, kind, new_ref, out_ref):
    count, _, width, shots = new_ref.shape
    rows = mask_ref.shape[3]
    for k in range(out_ref.shape[0]):
        chosen = jnp.zeros((2, width // rows, rows, shots), F32)
        for b in range(count):
            block = new_ref[b].reshape(chosen.shape)
            chosen = jnp.where(mask_ref[kind, k, b][None, None] > 0.5, block, chosen)
        out_ref[k] = chosen.reshape(2, width, shots)


def second_tick(matrix_ref, own_ref, arrived_refs, new_ref):
    blocks = [(x.astype(BF16), y.astype(BF16)) for x, y in gather(*arrived_refs)]
    stacked = operand(blocks)
    store(two_products(matrix_ref, slice(0, stacked.shape[0]), stacked), own_ref, new_ref)


def on_odd_layer():
    return lax.axis_index("layer") % 2 == 1


def odd_kernel(mask_ref, matrix_ref, own_ref, all_ref, even_ref, odd_ref, new_ref, new_even_ref, new_odd_ref):
    @pl.when(on_odd_layer())
    def _():
        second_tick(matrix_ref, own_ref, (all_ref, even_ref, odd_ref), new_ref)

    @pl.when(jnp.logical_not(on_odd_layer()))
    def _():
        new_ref[...] = own_ref[...]

    choose(mask_ref, 0, new_ref, new_even_ref)
    choose(mask_ref, 1, new_ref, new_odd_ref)


def on_even_layer():
    layer = lax.axis_index("layer")
    return (layer % 2 == 0) & (layer > 0)


def even_kernel(mask_ref, matrix_ref, own_ref, known_ref, all_ref, even_ref, odd_ref, new_ref, new_even_ref, new_odd_ref):
    @pl.when(jnp.logical_not(on_even_layer()))
    def _():
        new_ref[...] = known_ref[...]

    @pl.when(on_even_layer())
    def _():
        second_tick(matrix_ref, own_ref, (all_ref, even_ref, odd_ref), new_ref)

    choose(mask_ref, 0, new_ref, new_even_ref)
    choose(mask_ref, 1, new_ref, new_odd_ref)


def third_tick(matrix_ref, first, base_ref, refs, out_ref):
    blocks = gather(*refs)
    unit = 2 * base_ref.shape[2]
    columns = slice(first * unit, (first + len(blocks)) * unit)
    store(three_products(matrix_ref, columns, blocks), base_ref, out_ref)


def first_own_column(matrix_ref, trace_ref):
    blocks, _, width, _ = trace_ref.shape
    return matrix_ref.shape[1] // (2 * width) - blocks


def odd_own_kernel(matrix_ref, source_ref, trace_ref, payload_ref, out_ref, passed_ref):
    passed_ref[...] = payload_ref[...]

    @pl.when(on_odd_layer())
    def _():
        third_tick(matrix_ref, first_own_column(matrix_ref, trace_ref), source_ref, (trace_ref,), out_ref)

    @pl.when(jnp.logical_not(on_odd_layer()))
    def _():
        out_ref[...] = source_ref[...].astype(F32)


def pair_kernel(matrix_ref, base_ref, trace_ref, pair_ref, out_ref):
    @pl.when(on_odd_layer())
    def _():
        third_tick(matrix_ref, 0, base_ref, (pair_ref.at[0],), out_ref)

    @pl.when(jnp.logical_not(on_odd_layer()))
    def _():
        third_tick(matrix_ref, first_own_column(matrix_ref, trace_ref), base_ref, (trace_ref,), out_ref)


def even_part_kernel(matrix_ref, base_ref, all_ref, even_ref, out_ref, final_hbm, sem):
    @pl.when(lax.axis_index("layer") == 0)
    def _():
        copy = pltpu.make_async_copy(base_ref, final_hbm, sem)
        copy.start()
        copy.wait()

    @pl.when(on_odd_layer())
    def _():
        out_ref[...] = base_ref[...]

    @pl.when(on_even_layer())
    def _():
        third_tick(matrix_ref, 0, base_ref, (all_ref, even_ref), out_ref)


def last_kernel(
    matrix_ref, base_ref, outer_odd_ref, inner_even_ref, inner_odd_ref, begun_hbm, final_hbm, out_ref, sems
):
    blocks, _, width, shots = base_ref.shape

    def finish(first, refs):
        received = gather(*refs)
        halves = [(split(x), split(y)) for x, y in received]
        high = operand([(x[0], y[0]) for x, y in halves])
        low = operand([(x[1], y[1]) for x, y in halves])
        columns = slice(first * 2 * width, (first + len(received)) * 2 * width)
        copies = []
        for b in range(blocks):
            upper = matrix_ref[b * width : (b + 1) * width, columns]
            under = matrix_ref[(blocks + b) * width : (blocks + b + 1) * width, columns]
            result = product(upper, high) + product(under, high) + product(upper, low)
            for part in range(2):
                out_ref[b, part] = result[:, part * shots : (part + 1) * shots] + base_ref[b, part]
            copies.append(pltpu.make_async_copy(out_ref.at[b], final_hbm.at[b], sems.at[b]))
            copies[-1].start()
        for copy in copies:
            copy.wait()

    @pl.when(on_odd_layer())
    def _():
        finish(blocks, (inner_even_ref, inner_odd_ref))

    @pl.when(on_even_layer())
    def _():
        finish(blocks + inner_even_ref.shape[0], (outer_odd_ref,))


def call(kernel, ins, outs, flops, scratch=(), in_hbm=False, moved=None, last_in_hbm=False, last_out_hbm=False):
    if moved is None:
        moved = sum(x.size * x.dtype.itemsize for x in (*ins, *outs))
    vmem = pl.BlockSpec(memory_space=pltpu.VMEM)
    hbm = pl.BlockSpec(memory_space=pltpu.HBM)
    held = [in_hbm and not (x.ndim == 4 and x.dtype == F32) for x in ins]
    if last_in_hbm:
        held[-1] = True
    ins = [pltpu.with_memory_space_constraint(x, pltpu.HBM) if h else x for x, h in zip(ins, held)]
    out_specs = [vmem] * len(outs)
    if last_out_hbm:
        out_specs[-1] = hbm
        outs = (*outs[:-1], pltpu.HBM(outs[-1].shape, outs[-1].dtype))
    return pl.pallas_call(
        kernel,
        out_shape=outs,
        in_specs=[hbm if h else vmem for h in held],
        out_specs=out_specs,
        scratch_shapes=scratch,
        input_output_aliases={len(ins) - 1: len(outs) - 1} if last_in_hbm else {},
        compiler_params=pltpu.CompilerParams(vmem_limit_bytes=LIMIT),
        cost_estimate=pl.CostEstimate(flops=flops, bytes_accessed=moved, transcendentals=0),
    )(*ins)


def per_device(sources, operator_tiles, tile_rows, tile_cols, send_blocks):
    source = sources[0]
    tiles = operator_tiles[0]
    rows = tile_rows.reshape(-1)
    cols = tile_cols.reshape(-1)
    send = send_blocks.reshape(-1)
    blocks, _, width, shots = source.shape
    listed = send_blocks.shape[2]
    extended = 2 * blocks + 2 * listed
    shape = jax.ShapeDtypeStruct
    trace = shape(source.shape, F32)
    part = shape((listed, 2, width, shots), F32)
    matrix = shape((2 * blocks * width, extended * 2 * width), BF16)
    mask = shape((2, listed, blocks, 8, shots), F32)
    flops = 2 * blocks * width * extended * 2 * width * 2 * shots

    send_copy = pltpu.SMEM(send.shape, send.dtype)
    source_copy = pltpu.VMEM(source.shape, source.dtype)
    whole, even, odd = call(
        widen_kernel,
        (send, source),
        (trace, part, part),
        10**11,
        [send_copy, source_copy, pltpu.SemaphoreType.DMA((2,))],
        in_hbm=True,
        moved=10**8,
    )
    mate = permute(whole, inward, same)
    (later,) = call(after_kernel, (mate, even), (part,), 0)
    whole = permute(whole, outward, same)
    from_odd = permute(later, outward, even_pair), permute(odd, outward, odd_pair)
    from_even = permute(even, inward, even_pair), permute(odd, inward, odd_pair)
    matrix, own, mask = call(
        prepare_kernel,
        (rows, cols, send, source, tiles),
        (matrix, trace, mask),
        flops,
        [
            pltpu.SMEM(rows.shape, rows.dtype),
            pltpu.SMEM(cols.shape, cols.dtype),
            send_copy,
            pltpu.VMEM((blocks * extended, width, 2 * width), F32),
            pltpu.SemaphoreType.DMA((3,)),
        ],
    )
    second, even, odd = call(odd_kernel, (mask, matrix, own, mate, *from_even), (trace, part, part), flops)
    third, odd = call(odd_own_kernel, (matrix, source, second, odd), (trace, part), flops)
    early = permute(second, outward, same), permute(even, outward, even_pair), permute(odd, outward, odd_pair)
    traces, even, odd = call(
        even_kernel, (mask, matrix, own, second, whole, *from_odd), (trace, part, part), flops)
    late_even = permute(even, inward, even_pair)
    late_odd = permute(odd, inward, odd_pair)
    pair = with_mate(traces)
    (own,) = call(pair_kernel, (matrix, third, traces, pair), (trace,), flops)
    own, begun = call(
        even_part_kernel,
        (matrix, own, *early[:2]),
        (trace, trace),
        10**11,
        [pltpu.SemaphoreType.DMA],
        moved=10**9,
        last_out_hbm=True,
    )
    (out,) = call(
        last_kernel,
        (matrix, own, early[2], late_even, late_odd, begun),
        (trace,),
        flops,
        [pltpu.VMEM(trace.shape, F32), pltpu.SemaphoreType.DMA((blocks,))],
        last_in_hbm=True,
        last_out_hbm=True,
    )
    return out[None]


def solution(mesh):
    placed = (
        P("layer", "plane", None, None, None),
        P("layer", "plane", None, None, None),
        P("layer", "plane"),
        P("layer", "plane"),
        P("plane", None, None),
    )
    return jax.shard_map(
        per_device,
        mesh=mesh,
        in_specs=placed,
        out_specs=P("layer", "plane", None, None, None),
        check_vma=False,
    )
```

```python
import jax
import jax.numpy as jnp
from jax import lax
from jax.experimental import pallas as pl
from jax.experimental.pallas import tpu as pltpu
from jax.sharding import PartitionSpec as P

F32 = jnp.float32
BF16 = jnp.bfloat16
LIMIT = 40 * 1024 * 1024
LONG = 10**11


def even_pair(p, planes):
    q = p + 1 if p % 2 == 0 else p - 1
    return q if q < planes else p


def odd_pair(p, planes):
    q = p - 1 if p % 2 == 0 else p + 1
    return q if 0 <= q < planes else p


def same(p, planes):
    return p


def outward(l, p, layers, planes, partner):
    return (l + 1) % layers, partner(p, planes) if l % 2 == 1 and l + 1 < layers else p


def inward(l, p, layers, planes, partner):
    if l % 2 == 1:
        return l - 1, p
    return (l + 1, partner(p, planes)) if l + 1 < layers else (l, p)


def permute(block, way, partner):
    layers = lax.axis_size("layer")
    planes = lax.axis_size("plane")
    route = []
    for l in range(layers):
        for p in range(planes):
            to_layer, to_plane = way(l, p, layers, planes, partner)
            route.append((l * planes + p, to_layer * planes + to_plane))
    return lax.ppermute(block, ("layer", "plane"), route)


def with_mate(block):
    layers = lax.axis_size("layer")
    if layers % 2:
        return permute(block, inward, same)[None]
    groups = [[l, l + 1] for l in range(0, layers, 2)]
    return lax.all_gather(block, "layer", axis_index_groups=groups)


def split(value):
    high = value.astype(BF16)
    return high, (value - high.astype(F32)).astype(BF16)


def operand(blocks):
    rows = []
    for real, imag in blocks:
        rows.append(jnp.concatenate([real, imag], axis=1))
        rows.append(jnp.concatenate([-imag, real], axis=1))
    return jnp.concatenate(rows, axis=0)


def product(a, b):
    return jnp.dot(a, b, preferred_element_type=F32)


def two_products(matrix_ref, columns, operand_value):
    both = product(matrix_ref[:, columns], operand_value)
    half = both.shape[0] // 2
    return both[:half] + both[half:]


def three_products(matrix_ref, columns, blocks):
    halves = [(split(x), split(y)) for x, y in blocks]
    high = operand([(x[0], y[0]) for x, y in halves])
    low = operand([(x[1], y[1]) for x, y in halves])
    half = matrix_ref.shape[0] // 2
    return two_products(matrix_ref, columns, high) + product(matrix_ref[:half, columns], low)


def store(result, base_ref, out_ref):
    blocks, _, width, shots = base_ref.shape
    for b in range(blocks):
        for part in range(2):
            out_ref[b, part] = (
                result[b * width : (b + 1) * width, part * shots : (part + 1) * shots]
                + base_ref[b, part].astype(F32)
            )


def fetch(pairs, sems):
    copies = [pltpu.make_async_copy(a, b, sems.at[i]) for i, (a, b) in enumerate(pairs)]
    for copy in copies:
        copy.start()
    return copies


def widen_kernel(send_hbm, source_hbm, all_ref, even_ref, odd_ref, send_ref, source_ref, sems):
    copies = fetch([(source_hbm, source_ref), (send_hbm, send_ref)], sems)
    is_odd = lax.axis_index("plane") % 2
    listed = even_ref.shape[0]
    copies[0].wait()
    all_ref[...] = source_ref[...].astype(F32)
    copies[1].wait()
    for k in range(listed):
        even_ref[k] = source_ref[send_ref[(1 - is_odd) * listed + k]].astype(F32)
        odd_ref[k] = source_ref[send_ref[is_odd * listed + k]].astype(F32)


def after_kernel(first_ref, payload_ref, passed_ref):
    passed_ref[...] = payload_ref[...]


def prepare_kernel(
    rows_hbm, cols_hbm, send_hbm, source_hbm, tiles_ref,
    matrix_ref, own_ref, mask_ref,
    rows_ref, cols_ref, send_ref, source_ref, total, sems,
):
    tile_count, _, width, _ = tiles_ref.shape
    blocks_here = source_ref.shape[0]
    extended = total.shape[0] // blocks_here
    listed = (extended - 2 * blocks_here) // 2
    small = [(rows_hbm, rows_ref), (cols_hbm, cols_ref), (send_hbm, send_ref)]
    copies = fetch(small + [(source_hbm, source_ref)], sems)
    layer = lax.axis_index("layer")
    plane = lax.axis_index("plane")
    planes = lax.axis_size("plane")
    is_odd = plane % 2
    total[...] = jnp.zeros_like(total)

    def add(t, carry):
        col = cols_ref[t]
        is_lower = (col >= blocks_here) & (col < blocks_here + listed)
        is_upper = (col >= blocks_here + listed) & (col < blocks_here + 2 * listed)
        place = jnp.where(is_lower & (is_odd == 0), col + listed, col)
        place = jnp.where(is_upper & (is_odd == 0), col - listed, place)
        slot = rows_ref[t] * extended + place
        total[slot, :, :width] += tiles_ref[t, 0]
        total[slot, :, width:] += tiles_ref[t, 1]
        return carry

    for copy in copies[:3]:
        copy.wait()
    for k in range(listed):
        to_even = send_ref[(1 - is_odd) * listed + k]
        to_odd = send_ref[is_odd * listed + k]
        for b in range(blocks_here):
            for kind, chosen in enumerate((to_even, to_odd)):
                mask_ref[kind, k, b] = jnp.full(mask_ref.shape[3:], jnp.where(chosen == b, 1.0, 0.0), F32)
    lax.fori_loop(0, tile_count, add, 0, unroll=8)
    has_layer = layer > 0
    has_next = plane + 1 < planes
    has_even = has_layer & ((is_odd == 1) | has_next)
    has_odd = has_layer & jnp.where(is_odd == 1, has_next, plane > 0)
    height = blocks_here * width
    for c in range(extended):
        keep = None
        if c < blocks_here:
            keep = has_layer
        elif c < blocks_here + listed:
            keep = has_even
        elif c < blocks_here + 2 * listed:
            keep = has_odd
        for r in range(blocks_here):
            value = total[r * extended + c]
            if keep is not None:
                value = jnp.where(keep, value, 0.0)
            high, low = split(value)
            here = slice(c * 2 * width, (c + 1) * 2 * width)
            matrix_ref[r * width : (r + 1) * width, here] = high
            matrix_ref[height + r * width : height + (r + 1) * width, here] = low
    copies[-1].wait()
    own = operand([(source_ref[b, 0], source_ref[b, 1]) for b in range(blocks_here)])
    columns = slice((extended - blocks_here) * 2 * width, None)
    store(two_products(matrix_ref, columns, own), source_ref, own_ref)


def gather(*refs):
    return [(ref[b, 0], ref[b, 1]) for ref in refs for b in range(ref.shape[0])]


def choose(mask_ref, kind, new_ref, out_ref):
    count, _, width, shots = new_ref.shape
    rows = mask_ref.shape[3]
    for k in range(out_ref.shape[0]):
        chosen = jnp.zeros((2, width // rows, rows, shots), F32)
        for b in range(count):
            block = new_ref[b].reshape(chosen.shape)
            chosen = jnp.where(mask_ref[kind, k, b][None, None] > 0.5, block, chosen)
        out_ref[k] = chosen.reshape(2, width, shots)


def second_tick(matrix_ref, own_ref, arrived_refs, new_ref):
    blocks = [(x.astype(BF16), y.astype(BF16)) for x, y in gather(*arrived_refs)]
    stacked = operand(blocks)
    store(two_products(matrix_ref, slice(0, stacked.shape[0]), stacked), own_ref, new_ref)


def on_odd_layer():
    return lax.axis_index("layer") % 2 == 1


def odd_kernel(mask_ref, matrix_ref, own_ref, all_ref, even_ref, odd_ref, new_ref, new_even_ref, new_odd_ref):
    @pl.when(on_odd_layer())
    def _():
        second_tick(matrix_ref, own_ref, (all_ref, even_ref, odd_ref), new_ref)

    @pl.when(jnp.logical_not(on_odd_layer()))
    def _():
        new_ref[...] = own_ref[...]

    choose(mask_ref, 0, new_ref, new_even_ref)
    choose(mask_ref, 1, new_ref, new_odd_ref)


def on_even_layer():
    layer = lax.axis_index("layer")
    return (layer % 2 == 0) & (layer > 0)


def even_kernel(mask_ref, matrix_ref, own_ref, known_ref, all_ref, even_ref, odd_ref, new_ref, new_even_ref, new_odd_ref):
    @pl.when(jnp.logical_not(on_even_layer()))
    def _():
        new_ref[...] = known_ref[...]

    @pl.when(on_even_layer())
    def _():
        second_tick(matrix_ref, own_ref, (all_ref, even_ref, odd_ref), new_ref)

    choose(mask_ref, 0, new_ref, new_even_ref)
    choose(mask_ref, 1, new_ref, new_odd_ref)


def third_tick(matrix_ref, first, base_ref, refs, out_ref):
    blocks = gather(*refs)
    unit = 2 * base_ref.shape[2]
    columns = slice(first * unit, (first + len(blocks)) * unit)
    store(three_products(matrix_ref, columns, blocks), base_ref, out_ref)


def first_own_column(matrix_ref, trace_ref):
    blocks, _, width, _ = trace_ref.shape
    return matrix_ref.shape[1] // (2 * width) - blocks


def odd_own_kernel(matrix_ref, source_ref, trace_ref, payload_ref, out_ref, passed_ref):
    passed_ref[...] = payload_ref[...]

    @pl.when(on_odd_layer())
    def _():
        third_tick(matrix_ref, first_own_column(matrix_ref, trace_ref), source_ref, (trace_ref,), out_ref)

    @pl.when(jnp.logical_not(on_odd_layer()))
    def _():
        out_ref[...] = source_ref[...].astype(F32)


def pair_kernel(matrix_ref, base_ref, trace_ref, pair_ref, out_ref):
    @pl.when(on_odd_layer())
    def _():
        third_tick(matrix_ref, 0, base_ref, (pair_ref.at[0],), out_ref)

    @pl.when(jnp.logical_not(on_odd_layer()))
    def _():
        third_tick(matrix_ref, first_own_column(matrix_ref, trace_ref), base_ref, (trace_ref,), out_ref)


def even_part_kernel(matrix_ref, base_ref, all_ref, even_ref, out_ref, final_hbm, sem):
    @pl.when(lax.axis_index("layer") == 0)
    def _():
        copy = pltpu.make_async_copy(base_ref, final_hbm, sem)
        copy.start()
        copy.wait()

    @pl.when(on_odd_layer())
    def _():
        out_ref[...] = base_ref[...]

    @pl.when(on_even_layer())
    def _():
        third_tick(matrix_ref, 0, base_ref, (all_ref, even_ref), out_ref)


def last_kernel(
    matrix_ref, base_ref, outer_odd_ref, inner_even_ref, inner_odd_ref, begun_hbm, final_hbm, out_ref, sems
):
    blocks, _, width, shots = base_ref.shape

    def finish(first, refs):
        received = gather(*refs)
        halves = [(split(x), split(y)) for x, y in received]
        high = operand([(x[0], y[0]) for x, y in halves])
        low = operand([(x[1], y[1]) for x, y in halves])
        columns = slice(first * 2 * width, (first + len(received)) * 2 * width)
        copies = []
        for b in range(blocks):
            upper = matrix_ref[b * width : (b + 1) * width, columns]
            under = matrix_ref[(blocks + b) * width : (blocks + b + 1) * width, columns]
            result = product(upper, high) + product(under, high) + product(upper, low)
            for part in range(2):
                out_ref[b, part] = result[:, part * shots : (part + 1) * shots] + base_ref[b, part]
            copies.append(pltpu.make_async_copy(out_ref.at[b], final_hbm.at[b], sems.at[b]))
            copies[-1].start()
        for copy in copies:
            copy.wait()

    @pl.when(on_odd_layer())
    def _():
        finish(blocks, (inner_even_ref, inner_odd_ref))

    @pl.when(on_even_layer())
    def _():
        finish(blocks + inner_even_ref.shape[0], (outer_odd_ref,))


def call(kernel, ins, outs, flops, scratch=(), in_hbm=False, moved=None, last_in_hbm=False, last_out_hbm=False):
    if moved is None:
        moved = sum(x.size * x.dtype.itemsize for x in (*ins, *outs))
    vmem = pl.BlockSpec(memory_space=pltpu.VMEM)
    hbm = pl.BlockSpec(memory_space=pltpu.HBM)
    held = [in_hbm and not (x.ndim == 4 and x.dtype == F32) for x in ins]
    if last_in_hbm:
        held[-1] = True
    ins = [pltpu.with_memory_space_constraint(x, pltpu.HBM) if h else x for x, h in zip(ins, held)]
    out_specs = [vmem] * len(outs)
    if last_out_hbm:
        out_specs[-1] = hbm
        outs = (*outs[:-1], pltpu.HBM(outs[-1].shape, outs[-1].dtype))
    return pl.pallas_call(
        kernel,
        out_shape=outs,
        in_specs=[hbm if h else vmem for h in held],
        out_specs=out_specs,
        scratch_shapes=scratch,
        input_output_aliases={len(ins) - 1: len(outs) - 1} if last_in_hbm else {},
        compiler_params=pltpu.CompilerParams(vmem_limit_bytes=LIMIT),
        cost_estimate=pl.CostEstimate(flops=flops, bytes_accessed=moved, transcendentals=0),
    )(*ins)


def per_device(sources, operator_tiles, tile_rows, tile_cols, send_blocks):
    source = sources[0]
    tiles = operator_tiles[0]
    rows = tile_rows.reshape(-1)
    cols = tile_cols.reshape(-1)
    send = send_blocks.reshape(-1)
    blocks, _, width, shots = source.shape
    listed = send_blocks.shape[2]
    extended = 2 * blocks + 2 * listed
    shape = jax.ShapeDtypeStruct
    trace = shape(source.shape, F32)
    part = shape((listed, 2, width, shots), F32)
    matrix = shape((2 * blocks * width, extended * 2 * width), BF16)
    mask = shape((2, listed, blocks, 8, shots), F32)
    flops = 2 * blocks * width * extended * 2 * width * 2 * shots

    send_copy = pltpu.SMEM(send.shape, send.dtype)
    source_copy = pltpu.VMEM(source.shape, source.dtype)
    whole, even, odd = call(
        widen_kernel,
        (send, source),
        (trace, part, part),
        LONG,
        [send_copy, source_copy, pltpu.SemaphoreType.DMA((2,))],
        in_hbm=True,
        moved=10**8,
    )
    mate = permute(whole, inward, same)
    (later,) = call(after_kernel, (mate, even), (part,), 0)
    whole = permute(whole, outward, same)
    from_odd = permute(later, outward, even_pair), permute(odd, outward, odd_pair)
    from_even = permute(even, inward, even_pair), permute(odd, inward, odd_pair)
    matrix, own, mask = call(
        prepare_kernel,
        (rows, cols, send, source, tiles),
        (matrix, trace, mask),
        flops,
        [
            pltpu.SMEM(rows.shape, rows.dtype),
            pltpu.SMEM(cols.shape, cols.dtype),
            send_copy,
            source_copy,
            pltpu.VMEM((blocks * extended, width, 2 * width), F32),
            pltpu.SemaphoreType.DMA((4,)),
        ],
        in_hbm=True,
    )
    second, even, odd = call(odd_kernel, (mask, matrix, own, mate, *from_even), (trace, part, part), flops)
    third, odd = call(odd_own_kernel, (matrix, source, second, odd), (trace, part), flops)
    early = permute(second, outward, same), permute(even, outward, even_pair), permute(odd, outward, odd_pair)
    traces, even, odd = call(
        even_kernel, (mask, matrix, own, second, whole, *from_odd), (trace, part, part), flops
    )
    late_even = permute(even, inward, even_pair)
    late_odd = permute(odd, inward, odd_pair)
    pair = with_mate(traces)
    (own,) = call(pair_kernel, (matrix, third, traces, pair), (trace,), flops)
    own, begun = call(
        even_part_kernel,
        (matrix, own, *early[:2]),
        (trace, trace),
        LONG,
        [pltpu.SemaphoreType.DMA],
        moved=10**9,
        last_out_hbm=True,
    )
    (out,) = call(
        last_kernel,
        (matrix, own, early[2], late_even, late_odd, begun),
        (trace,),
        flops,
        [pltpu.VMEM(trace.shape, F32), pltpu.SemaphoreType.DMA((blocks,))],
        last_in_hbm=True,
        last_out_hbm=True,
    )
    return out[None]


def solution(mesh):
    placed = (
        P("layer", "plane", None, None, None),
        P("layer", "plane", None, None, None),
        P("layer", "plane"),
        P("layer", "plane"),
        P("plane", None, None),
    )
    return jax.shard_map(
        per_device,
        mesh=mesh,
        in_specs=placed,
        out_specs=P("layer", "plane", None, None, None),
        check_vma=False,
    )
```
